32 devices in a mesh: groups: 2 (over x), tile: 16 (over z, y, core).
Axes of the slice: x: 2, y: 2, z: 4, core: 2. Of those that a mesh axis runs over, the one named last changes fastest.
Arguments:
- log_conductivity: float32 [4, 128, 1024], P('groups', 'tile'), parts along dimension 0, may hold values from -2.9 to 3, as said below
- storage: float32 [4, 128, 1024], P('groups', 'tile'), parts along dimension 0, may hold values from 0.05 to 60
- recharge: float32 [4, 128, 1024], P('groups', 'tile'), parts along dimension 0, may hold values from -6 to 6
- observed: float32 [24, 400], P('groups'), parts along dimension 0, may hold values from -6 to 6
- rates: float32 [24], P('groups'), parts along dimension 0, may hold values from 2 to 8
- well_tile: int32 [400], replicated, may hold values from 0 to 15
- well_row: int32 [400], replicated, may hold values from 0 to 7
- well_col: int32 [400], replicated, may hold values from 0 to 1023
- well_screen: int32 [400, 2], replicated, may hold values from 0 to 2, as said below
- test_well: int32 [12], replicated, may hold values from 0 to 399
Outputs:
- gradient: float32 [4, 128, 1024], P('groups', 'tile'), parts along dimension 0
- predicted: float32 [24, 400], P('groups'), parts along dimension 0
The draws below stay inside these ranges and needn't reach their ends.
There are 2 independent parts, one for each index of `groups`. The reference program is written for one: setup_inputs(seed, part) draws one part's arguments, and reference() takes and returns one part's arrays. A program takes and returns all parts, laid end to end along the dimension named above; an argument that names none is the same for every part. Nothing has to cross between parts.
Inputs may be any that keep to these rules, and one draw needn't show every extreme that they name: `log_conductivity`: log-conductivities rough from cell to cell. Each well's screen holds one or more whole layers, well_screen[w,0] < well_screen[w,1].
All inputs are finite; a program needn't handle non-finite values.
Results may differ from the reference program's by a relative error of at most 0.00014.
Values sent between devices are 32-bit elements; how exact they have to be, the bound alone decides.
A program may use at most 64 MiB of HBM per device.

```python
import math
import jax
import jax.numpy as jnp
import numpy as np
from jax import lax

NL = 2
CX = 8
NY = 1024
TESTS = 12
NW = 400
ITERS = 4
NX = 128
N_TILE = 16


def draw_log_conductivity(key, part):
    positions = jnp.arange(NX, dtype=jnp.float32) / NX
    trend = math.log(3.0) * positions[None, :, None] - 0.5
    noise = jnp.clip(0.8 * jax.random.normal(key, (NL, NX, NY), jnp.float32), -2.4, 2.4)
    return (noise + trend).astype(jnp.float32)


def draw_storage(key, part):
    positions = jnp.arange(NX, dtype=jnp.float32) / NX
    trend = jnp.exp(-math.log(3.0) * positions)[None, :, None]
    key_level = jax.random.fold_in(key, 5)
    key_depth = jax.random.fold_in(key, 7)
    key_place = jax.random.fold_in(key, 9)
    level = jnp.exp(jax.random.uniform(key_level, (), jnp.float32, math.log(2.0), math.log(30.0)))
    depth = jnp.exp(jax.random.uniform(key_depth, (), jnp.float32, math.log(0.15), math.log(0.5)))
    place = jax.random.randint(key_place, (), 0, NX)
    spot = jnp.where(jnp.arange(NX, dtype=jnp.int32) == place, depth, jnp.float32(1.0))[None, :, None]
    noise = jnp.exp(jax.random.uniform(key, (NL, NX, NY), jnp.float32, math.log(0.5), math.log(2.0)))
    return (noise * trend * level * spot).astype(jnp.float32)


def draw_well_screen(key, part):
    key_top = jax.random.fold_in(key, 11)
    key_len = jax.random.fold_in(key, 23)
    top = jax.random.randint(key_top, (NW,), 0, NL)
    length = 1 + jax.random.randint(key_len, (NW,), 0, NL - top)
    top = top.at[0].set(0)
    length = length.at[0].set(NL)
    return jnp.stack((top, top + length), axis=1).astype(jnp.int32)


def plant(entries, own_key, least, high):
    spot = [jax.random.randint(jax.random.fold_in(own_key, axis), (), 0, length) for axis, length in enumerate(entries.shape)]
    longest = entries.shape.index(max(entries.shape))
    beside = spot[:longest] + [(spot[longest] + 1) % entries.shape[longest]] + spot[longest + 1:]
    return entries.at[tuple(spot)].set(least).at[tuple(beside)].set(high)


def shard_levels(key, shape, pieces, least, top_value):
    gain, own = 1.0, jax.random.fold_in(key, 6)
    for dim, blocks in pieces:
        heights = jnp.exp(jax.random.uniform(jax.random.fold_in(own, dim), (blocks,), jnp.float32, least / len(pieces), top_value / len(pieces)))
        gain = gain * jnp.repeat(heights, shape[dim] // blocks).reshape([-1 if axis == dim else 1 for axis in range(len(shape))])
    return gain


def cumulative_ranks(amount, lean):
    weights = [(1 << 20) // math.isqrt(grade ** lean) + 1 for grade in range(1, amount + 1)]
    deviation = 1 + sum(weights) // (1 << 30)
    return np.cumsum(np.array([max(1, weight // deviation) for weight in weights]))


def ranked(key, dims, amount, slope):
    table = cumulative_ranks(amount, slope)
    pick = jax.random.randint(jax.random.fold_in(key, 1), dims, 0, int(table[amount - 1]))
    rank = jnp.searchsorted(jnp.asarray(table, jnp.int32), pick, side="right")
    return jax.random.permutation(jax.random.fold_in(key, 2), amount)[rank].astype(jnp.int32)


def normal_values(rng, shape, scale, most, shards=(), held_as=jnp.bfloat16):
    entries = jax.random.normal(rng, shape, jnp.float32) * scale
    if len(shards) > 0:
        entries = shard_levels(rng, shape, shards, -0.22, 0.18) * entries
    return jnp.clip(entries, min=-most, max=most).astype(held_as)


def setup_inputs(seed: int = 0, part: int = 0) -> dict:
    keys = jax.random.split(jax.random.key(seed), 11)
    own_keys = jax.random.split(jax.random.fold_in(keys[10], part), 11)
    log_conductivity = draw_log_conductivity(jax.random.fold_in(jax.random.fold_in(keys[10], part), 71), part)
    storage = draw_storage(jax.random.fold_in(jax.random.fold_in(keys[10], part), 71), part)
    recharge = normal_values(own_keys[2], (NL, NX, NY), 1.0, 6.0, ((1, 16),), jnp.float32)
    observed = normal_values(own_keys[3], (TESTS, NW), 1.0, 6.0, (), jnp.float32)
    rates = jnp.clip(jnp.exp(jax.random.uniform(own_keys[4], (TESTS,), jnp.float32, math.log(2.0), math.log(8.0))), 2.0, 8.0)
    well_tile = plant(ranked(keys[5], (NW,), N_TILE, 2), jax.random.fold_in(keys[5], 3), 0, N_TILE - 1).astype(jnp.int32)
    well_row = plant(jax.random.randint(keys[6], (NW,), 0, CX), jax.random.fold_in(keys[6], 1), 0, CX - 1).astype(jnp.int32)
    well_col = plant(jax.random.randint(keys[7], (NW,), 0, NY), jax.random.fold_in(keys[7], 1), 0, NY - 1).astype(jnp.int32)
    well_screen = draw_well_screen(jax.random.fold_in(keys[10], 71), part)
    test_well = plant(jax.random.randint(keys[9], (TESTS,), 0, NW), jax.random.fold_in(keys[9], 1), 0, NW - 1).astype(jnp.int32)
    return dict(log_conductivity=log_conductivity, storage=storage, recharge=recharge, observed=observed, rates=rates, well_tile=well_tile, well_row=well_row, well_col=well_col, well_screen=well_screen, test_well=test_well)


def pad_axis(array, axis, before, after):
    widths = [(0, 0)] * array.ndim
    widths[axis] = (before, after)
    return jnp.pad(array, widths)

def faces_of(conductivity):
    padded_x = pad_axis(conductivity, 1, 1, 1)
    faces_x = 0.5 * (padded_x[:, 1:, :] + padded_x[:, :-1, :])
    padded_y = pad_axis(conductivity, 2, 1, 1)
    faces_y = 0.5 * (padded_y[:, :, 1:] + padded_y[:, :, :-1])
    faces_z = 0.5 * (conductivity[1:] + conductivity[:-1])
    return (faces_x, faces_y, faces_z)

def operate(padded, faces_x, faces_y, faces_z, store):
    field = padded[..., 1:-1, :]
    flux_x = faces_x * (padded[..., 1:, :] - padded[..., :-1, :])
    result = store * field + flux_x[..., :-1, :] - flux_x[..., 1:, :]
    padded_y = pad_axis(field, field.ndim - 1, 1, 1)
    flux_y = faces_y * (padded_y[..., 1:] - padded_y[..., :-1])
    result = result + flux_y[..., :-1] - flux_y[..., 1:]
    flux_z = faces_z * (field[..., 1:, :, :] - field[..., :-1, :, :])
    layer_axis = field.ndim - 3
    return result + pad_axis(flux_z, layer_axis, 1, 0) - pad_axis(flux_z, layer_axis, 0, 1)

def chebyshev(source, apply_op, low, high):
    center = 0.5 * (high + low)
    radius = 0.5 * (high - low)
    spread = center / radius
    ratio = 1.0 / spread
    direction = source / center
    iterate = direction
    residual = source
    for turn in range(ITERS):
        residual = residual - apply_op(direction)
        ratio_next = 1.0 / (2.0 * spread - ratio)
        direction = ratio_next * ratio * direction + 2.0 * ratio_next / radius * residual
        iterate = iterate + direction
        ratio = ratio_next
    return iterate

def reference(log_conductivity, storage, recharge, observed, rates, well_tile, well_row, well_col, well_screen, test_well):
    conductivity = jnp.exp(log_conductivity)
    faces_x, faces_y, faces_z = faces_of(conductivity)
    face_sum = faces_x[:, :-1] + faces_x[:, 1:] + faces_y[:, :, :-1] + faces_y[:, :, 1:]
    face_sum = face_sum + pad_axis(faces_z, 0, 1, 0) + pad_axis(faces_z, 0, 0, 1)
    high = jnp.max(storage + 2.0 * face_sum)
    low = jnp.min(storage)

    def apply_op(field):
        return operate(pad_axis(field, 1, 1, 1), faces_x, faces_y, faces_z, storage)
    layers = jnp.arange(NL, dtype=jnp.int32)
    top = well_screen[:, 0]
    bottom = well_screen[:, 1]
    inside = ((layers[None, :] >= top[:, None]) & (layers[None, :] < bottom[:, None])).astype(jnp.float32)
    screen_weight = inside / (bottom - top).astype(jnp.float32)[:, None]
    first_index = (well_tile * CX + well_row).astype(jnp.int32)

    def solve_heads(test):
        pumped = test_well[test]
        source = recharge.at[:, first_index[pumped], well_col[pumped]].add(-rates[test] * screen_weight[pumped])
        return chebyshev(source, apply_op, low, high)

    def predict(test):
        heads = solve_heads(test)
        return lax.optimization_barrier(jnp.sum(heads[:, first_index, well_col] * screen_weight.T, axis=0))
    predicted = lax.map(predict, jnp.arange(TESTS, dtype=jnp.int32))
    misfit = predicted - observed
    scale = jnp.sqrt(jnp.mean(misfit * misfit) + 1e-06)
    weight = misfit / scale

    def accumulate(total, test):
        heads = solve_heads(test)
        adjoint_source = jnp.zeros_like(recharge).at[:, first_index, well_col].add((weight[test][:, None] * screen_weight).T)
        adjoint = chebyshev(adjoint_source, apply_op, low, high)
        padded_a = pad_axis(adjoint, 1, 1, 1)
        padded_h = pad_axis(heads, 1, 1, 1)
        term_x = 0.5 * (padded_a[:, 1:] - padded_a[:, :-1]) * (padded_h[:, 1:] - padded_h[:, :-1])
        padded_a = pad_axis(adjoint, 2, 1, 1)
        padded_h = pad_axis(heads, 2, 1, 1)
        term_y = 0.5 * (padded_a[:, :, 1:] - padded_a[:, :, :-1]) * (padded_h[:, :, 1:] - padded_h[:, :, :-1])
        term_z = 0.5 * (adjoint[1:] - adjoint[:-1]) * (heads[1:] - heads[:-1])
        cell_sum = term_x[:, :-1] + term_x[:, 1:] + term_y[:, :, :-1] + term_y[:, :, 1:]
        cell_sum = cell_sum + pad_axis(term_z, 0, 1, 0) + pad_axis(term_z, 0, 0, 1)
        return (total + cell_sum, 0.0)
    total, unused = lax.scan(accumulate, jnp.zeros_like(recharge), jnp.arange(TESTS, dtype=jnp.int32))
    gradient = -conductivity * total
    return (gradient, predicted)
```

```python
import functools

import jax
import jax.numpy as jnp
from jax import lax
from jax.experimental import pallas as pl
from jax.experimental.pallas import tpu as pltpu
from jax.sharding import PartitionSpec as P

ITERS = 4
HALF = 2 * ITERS + 2
WINDOW = 2 * HALF + 1
F32 = jnp.float32
BF16 = jnp.bfloat16
NT = (((1,), (1,)), ((), ()))
NN = (((1,), (0,)), ((), ()))
TN = (((0,), (0,)), ((), ()))


def split3(x):
    high = x.astype(BF16)
    rest = x - high.astype(F32)
    mid = rest.astype(BF16)
    low = (rest - mid.astype(F32)).astype(BF16)
    return high, mid, low


def mxu(a, b, dims):
    return lax.dot_general(a, b, dims, preferred_element_type=F32)


def exact_left(x, picks, dims):
    parts = [mxu(part, picks, dims) for part in split3(x)]
    return (parts[2] + parts[1]) + parts[0]


def exact_right(picks, x, dims):
    parts = [mxu(picks, part, dims) for part in split3(x)]
    return (parts[2] + parts[1]) + parts[0]


def iota(shape, dim):
    return lax.broadcasted_iota(jnp.int32, shape, dim)


def turn(x, shift, axis):
    return pltpu.roll(x, shift % x.shape[axis], axis)


def kernel(
    n, tests, wells, rates_s, test_s,
    logc_ref, store_ref, rech_ref, obs_ref, tile_ref, row_ref, col_ref, screen_ref,
    grad_ref, pred_ref,
    halo, info, picks, near, coef, heads_ref, bounds, part, stage, full, obs_pad,
    halo_send, halo_recv, hl_send, hl_recv, red_send, red_recv, out_send, out_recv,
):
    layers, strip, columns = logc_ref.shape
    assert layers == 2
    rows = 3 * strip
    both = layers * rows
    wide = info.shape[1]
    wpad = near.shape[0]
    packed = near.shape[1]
    lanes = columns + packed
    me = lax.axis_index("tile")

    barrier = pltpu.get_barrier_semaphore()
    for k in range(1, n):
        pl.semaphore_signal(
            barrier, inc=1, device_id={"tile": lax.rem(me + k, n)},
            device_id_type=pl.DeviceIdType.MESH,
        )
    pl.semaphore_wait(barrier, n - 1)

    def halo_copy(side, index):
        ref = (logc_ref, store_ref, rech_ref)[index]
        target = me + 1 if side == 0 else me - 1
        return pltpu.make_async_remote_copy(
            src_ref=ref, dst_ref=halo.at[side, index],
            send_sem=halo_send.at[side, index], recv_sem=halo_recv.at[side, index],
            device_id={"tile": target}, device_id_type=pl.DeviceIdType.MESH,
        )

    fills = (-1e30, 0.0, 0.0)
    for side, sends, gets in ((0, me < n - 1, me > 0), (1, me > 0, me < n - 1)):
        @pl.when(sends)
        def _():
            for index in range(3):
                halo_copy(side, index).start()

        @pl.when(jnp.logical_not(gets))
        def _():
            for index in range(3):
                halo[side, index] = jnp.full((layers, strip, columns), fills[index], F32)

    info[...] = jnp.full(info.shape, -4000.0, F32)
    info[0:1, 0:wells] = col_ref[...].astype(F32)
    info[1:2, 0:wells] = ((tile_ref[...] - me) * strip + row_ref[...] + strip).astype(F32)
    info[2:4, 0:wells] = screen_ref[...].astype(F32)
    well_col = info[0:1, 0:wpad]
    well_row = info[1:2, 0:wpad]
    top = info[2:3, 0:wpad]
    bottom = info[3:4, 0:wpad]
    length = jnp.where(bottom > top, bottom - top, 1.0)
    screens = [
        jnp.where((top <= layer) & (bottom > layer), 1.0 / length, 0.0) for layer in range(layers)
    ]
    trow = iota((16, 1), 0)
    pumped = jnp.full((16, 1), -1, jnp.int32)
    rate = jnp.zeros((16, 1), F32)
    for t in range(tests):
        pumped = jnp.where(trow == t, test_s[t], pumped)
        rate = jnp.where(trow == t, rates_s[t], rate)
    chosen = iota((16, wpad), 1) == pumped

    def at_pumped(values):
        return jnp.sum(jnp.where(chosen, values, 0.0), axis=1, keepdims=True)

    slot = iota((16, packed), 1) - WINDOW * trow
    segment = (slot >= 0) & (slot < WINDOW) & (trow < tests)

    def to_lanes(column):
        return jnp.sum(jnp.where(segment, column, 0.0), axis=0, keepdims=True)

    label = jnp.sum(
        jnp.where(segment, at_pumped(well_col) - HALF + slot.astype(F32), 0.0),
        axis=0, keepdims=True,
    )
    label = jnp.where(iota((1, packed), 1) < tests * WINDOW, label, -2000.0)
    info[0:1, wpad:] = label
    pump_row = to_lanes(at_pumped(well_row))
    centre = segment & (slot == HALF)
    amounts = [
        jnp.sum(jnp.where(centre, -rate * at_pumped(screen), 0.0), axis=0, keepdims=True)
        for screen in screens
    ]
    line = iota((rows, 1), 0).astype(F32)
    pumping = jnp.concatenate(
        [jnp.where(line == pump_row, amount, 0.0) for amount in amounts], axis=0
    )
    rowsel = jnp.concatenate(
        [jnp.where(line == well_row, screen, 0.0) for screen in screens], axis=0
    )
    upright = info[...].T[:, 0:1]
    picks[...] = jnp.where(
        upright == iota((wide, columns), 1).astype(F32), 1.0, 0.0
    ).astype(BF16)
    near[...] = jnp.where(upright[0:wpad] == label, 1.0, 0.0)
    obs_pad[...] = jnp.zeros(obs_pad.shape, F32)
    obs_pad[0:tests, 0:wells] = obs_ref[...]

    for side, gets in ((0, me > 0), (1, me < n - 1)):
        @pl.when(gets)
        def _():
            for index in range(3):
                halo_copy(side, index).wait_recv()

    def extended(ref, index):
        return jnp.concatenate(
            [
                piece
                for layer in range(layers)
                for piece in (halo[0, index, layer], ref[layer], halo[1, index, layer])
            ],
            axis=0,
        )

    cond = jnp.exp(extended(logc_ref, 0))
    store = extended(store_ref, 1)
    line2 = lax.rem(iota((both, 1), 0), rows)
    whole_row = line2 + (me - 1) * strip
    linked = (line2 >= 1) & (whole_row >= 1) & (whole_row < n * strip)
    column = iota((1, columns), 1)
    face_up = 0.5 * (cond + turn(cond, 1, 0))
    up = jnp.where(linked, face_up, 0.0)
    left_open = 0.5 * (cond + turn(cond, 1, 1))
    left = jnp.where(column == 0, 0.0, left_open)
    face_left = jnp.where(column == 0, 0.5 * cond, left_open)
    face_right = jnp.where(column == columns - 1, 0.5 * cond, turn(left_open, -1, 1))
    across = 0.5 * (cond + turn(cond, rows, 0))
    faces = face_up + turn(face_up, -1, 0) + face_left + face_right + across
    diag = store + faces

    def own(x):
        return jnp.concatenate(
            [x[layer * rows + strip:layer * rows + 2 * strip] for layer in range(layers)], axis=0
        )

    high_own = jnp.max(own(store + 2.0 * faces), keepdims=True)
    low_own = jnp.min(own(store), keepdims=True)
    bounds[0] = jnp.where(iota((1, 128), 1) < 64, high_own, -low_own)

    def bound_copy(k):
        return pltpu.make_async_remote_copy(
            src_ref=bounds.at[0], dst_ref=bounds.at[k],
            send_sem=hl_send.at[k], recv_sem=hl_recv.at[k],
            device_id={"tile": lax.rem(me + k, n)}, device_id_type=pl.DeviceIdType.MESH,
        )

    for k in range(1, n):
        bound_copy(k).start()

    stacked = jnp.concatenate([diag, up, left, across], axis=0)
    taken = exact_left(stacked, picks[wpad:, :], NT)
    for index, whole in enumerate((diag, up, left, across)):
        coef[index, :, 0:columns] = whole
        coef[index, :, columns:] = taken[index * both:(index + 1) * both]
    coef[2, :, columns:columns + 128] = jnp.where(
        iota((1, 128), 1) == 0, 0.0, taken[2 * both:3 * both, 0:128]
    )

    def operate(v):
        out = coef[0] * v - coef[1] * turn(v, 1, 0) - turn(coef[1] * v, -1, 0)
        out = out - coef[2] * turn(v, 1, 1) - turn(coef[2] * v, -1, 1)
        return out - coef[3] * turn(v, rows, 0)

    source = jnp.concatenate([extended(rech_ref, 2), pumping], axis=1)
    applied = operate(source)

    for k in range(1, n):
        bound_copy(k).wait_recv()
    bound = jnp.max(bounds[...], axis=0)
    high = bound[:, 0:1]
    low = -bound[:, 64:65]
    center = 0.5 * (high + low)
    radius = 0.5 * (high - low)
    spread = center / radius

    def chebyshev(source, applied):
        ratio = 1.0 / spread
        direction = source / center
        iterate = direction
        residual = source
        for step in range(ITERS):
            if step == 0:
                residual = residual - applied / center
            else:
                residual = residual - operate(direction)
            following = 1.0 / (2.0 * spread - ratio)
            direction = (following * ratio) * direction + (2.0 * following / radius) * residual
            iterate = iterate + direction
            ratio = following
        return iterate

    heads = chebyshev(source, applied)
    heads_ref[...] = heads
    mine = own(heads)
    rowsel_own = own(rowsel)
    common = jnp.sum(
        exact_left(mine[:, 0:columns], picks[0:wpad, :], NT) * rowsel_own, axis=0, keepdims=True
    )
    deltas = mine[:, columns:]
    place = iota((1, packed), 1)
    spaced = jnp.concatenate(
        [
            jnp.where((place >= t * WINDOW) & (place < (t + 1) * WINDOW), deltas, 0.0)
            for t in range(tests)
        ],
        axis=0,
    )
    read = exact_left(spaced, near[...].astype(BF16), NT)
    depth = layers * strip
    sampled = [
        jnp.sum(read[t * depth:(t + 1) * depth] * rowsel_own, axis=0, keepdims=True) + common
        for t in range(tests)
    ]
    sampled = jnp.concatenate(sampled + [jnp.zeros((16 - tests, wpad), F32)], axis=0)
    across_tiles = wpad // 128
    tiles = 2 * across_tiles
    gap = n // tiles
    for k in range(tiles):
        r, c = 8 * (k // across_tiles), 128 * (k % across_tiles)
        part[k] = sampled[r:r + 8, c:c + 128]

    def to_reducer(k):
        order = lax.rem(me - k * gap + n, n)
        return pltpu.make_async_remote_copy(
            src_ref=part.at[k], dst_ref=stage.at[order],
            send_sem=red_send.at[k], recv_sem=red_recv.at[order],
            device_id={"tile": k * gap}, device_id_type=pl.DeviceIdType.MESH,
        )

    def from_reducer(k, step):
        return pltpu.make_async_remote_copy(
            src_ref=full.at[k], dst_ref=full.at[k],
            send_sem=out_send.at[step], recv_sem=out_recv.at[k],
            device_id={"tile": lax.rem(me + step, n)}, device_id_type=pl.DeviceIdType.MESH,
        )

    def gathered(order):
        return pltpu.make_async_remote_copy(
            src_ref=part.at[0], dst_ref=stage.at[order],
            send_sem=red_send.at[0], recv_sem=red_recv.at[order],
            device_id={"tile": me}, device_id_type=pl.DeviceIdType.MESH,
        )

    for k in range(tiles):
        @pl.when(me != k * gap)
        def _():
            to_reducer(k).start()

    for k in range(tiles):
        @pl.when(me == k * gap)
        def _():
            for order in range(1, n):
                gathered(order).wait_recv()
            stage[0] = part[k]
            full[k] = jnp.sum(stage[...], axis=0)
            for step in range(1, n):
                from_reducer(k, step).start()

    for k in range(tiles):
        @pl.when(me != k * gap)
        def _():
            from_reducer(k, 1).wait_recv()

    predicted = jnp.concatenate(
        [
            jnp.concatenate([full[r * across_tiles + c] for c in range(across_tiles)], axis=1)
            for r in range(2)
        ],
        axis=0,
    )
    pred_ref[...] = predicted[0:tests, 0:wells]
    valid = (iota((16, wpad), 0) < tests) & (iota((16, wpad), 1) < wells)
    misfit = jnp.where(valid, predicted - obs_pad[...], 0.0)
    total = jnp.sum(misfit * misfit, keepdims=True)
    weight = misfit / jnp.sqrt(total / (tests * wells) + 1e-06)

    summed = jnp.sum(weight, axis=0, keepdims=True)
    dense = exact_left(rowsel * summed, picks[0:wpad, :], NN)
    segment_f = jnp.where(segment, 1.0, 0.0).astype(BF16)
    spread_weight = exact_left(weight, segment_f, TN)
    placed = exact_right(rowsel.astype(BF16), spread_weight * near[...], NN)
    source = jnp.concatenate([dense, placed], axis=1)
    adjoint = chebyshev(source, operate(source))

    heads = heads_ref[...]
    lane = iota((1, lanes), 1)
    start = (lane == 0) | (lane == columns)

    def before(x):
        return jnp.where(start, 0.0, turn(x, 1, 1))

    term_x = 0.5 * (adjoint - turn(adjoint, 1, 0)) * (heads - turn(heads, 1, 0))
    x_sum = term_x + turn(term_x, -1, 0)
    term_y = 0.5 * (adjoint - before(adjoint)) * (heads - before(heads))
    term_right = jnp.where(
        lane == columns - 1, 0.5 * adjoint * heads, turn(term_y, -1, 1)
    )
    term_z = 0.5 * (adjoint - turn(adjoint, rows, 0)) * (heads - turn(heads, rows, 0))
    cells = own(x_sum + term_y + term_right + term_z)
    cells = cells[:, 0:columns] + exact_left(cells[:, columns:], picks[wpad:, :], NN)
    for layer in range(layers):
        grad_ref[layer] = -jnp.exp(logc_ref[layer]) * cells[layer * strip:(layer + 1) * strip]

    for side, sends in ((0, me < n - 1), (1, me > 0)):
        @pl.when(sends)
        def _():
            for index in range(3):
                halo_copy(side, index).wait_send()
    for k in range(1, n):
        bound_copy(k).wait_send()
    for k in range(tiles):
        @pl.when(me != k * gap)
        def _():
            to_reducer(k).wait_send()

        @pl.when(me == k * gap)
        def _():
            for step in range(1, n):
                from_reducer(k, step).wait_send()


def round_up(value, unit):
    return -(-value // unit) * unit


def local(
    log_conductivity, storage, recharge, observed, rates,
    well_tile, well_row, well_col, well_screen, test_well,
):
    layers, strip, columns = log_conductivity.shape
    tests, wells = observed.shape
    n = lax.axis_size("tile")
    wpad = round_up(wells, 128)
    packed = round_up(tests * WINDOW, 128)
    both = layers * 3 * strip
    lanes = columns + packed
    tiles = 2 * (wpad // 128)
    vmem = pl.BlockSpec(memory_space=pltpu.VMEM)
    smem = pl.BlockSpec(memory_space=pltpu.SMEM)
    dma = pltpu.SemaphoreType.DMA
    return pl.pallas_call(
        functools.partial(kernel, n, tests, wells),
        out_shape=(
            jax.ShapeDtypeStruct((layers, strip, columns), F32),
            jax.ShapeDtypeStruct((tests, wells), F32),
        ),
        in_specs=[smem, smem] + [vmem] * 8,
        out_specs=(vmem, vmem),
        scratch_shapes=[
            pltpu.VMEM((2, 3, layers, strip, columns), F32),
            pltpu.VMEM((8, wpad + packed), F32),
            pltpu.VMEM((wpad + packed, columns), BF16),
            pltpu.VMEM((wpad, packed), F32),
            pltpu.VMEM((4, both, lanes), F32),
            pltpu.VMEM((both, lanes), F32),
            pltpu.VMEM((n, 1, 128), F32),
            pltpu.VMEM((tiles, 8, 128), F32),
            pltpu.VMEM((n, 8, 128), F32),
            pltpu.VMEM((tiles, 8, 128), F32),
            pltpu.VMEM((16, wpad), F32),
            dma((2, 3)), dma((2, 3)), dma((n,)), dma((n,)),
            dma((tiles,)), dma((n,)), dma((n,)), dma((tiles,)),
        ],
        compiler_params=pltpu.CompilerParams(
            collective_id=0, has_side_effects=True, vmem_limit_bytes=40 * 1024 * 1024
        ),
    )(
        rates, test_well, log_conductivity, storage, recharge, observed,
        well_tile.reshape(1, wells), well_row.reshape(1, wells), well_col.reshape(1, wells),
        well_screen.T,
    )


def solution(mesh):
    return jax.shard_map(
        local,
        mesh=mesh,
        in_specs=(
            P("groups", "tile", None),
            P("groups", "tile", None),
            P("groups", "tile", None),
            P("groups", None),
            P("groups"),
            P(),
            P(),
            P(),
            P(),
            P(),
        ),
        out_specs=(P("groups", "tile", None), P("groups", None)),
        check_vma=False,
    )
```

```python
import functools

import jax
import jax.numpy as jnp
from jax import lax
from jax.experimental import pallas as pl
from jax.experimental.pallas import tpu as pltpu
from jax.sharding import PartitionSpec as P

ITERS = 4
HALF = 2 * ITERS + 2
WINDOW = 2 * HALF + 1
F32 = jnp.float32
BF16 = jnp.bfloat16
NT = (((1,), (1,)), ((), ()))
NN = (((1,), (0,)), ((), ()))
TN = (((0,), (0,)), ((), ()))


def split(x):
    high = x.astype(BF16)
    return high, (x - high.astype(F32)).astype(BF16)


def mxu(a, b, dims):
    return lax.dot_general(a, b, dims, preferred_element_type=F32)


def exact_left(x, picks, dims):
    both = mxu(jnp.concatenate(split(x), axis=0), picks, dims)
    return both[:x.shape[0]] + both[x.shape[0]:]


def exact_right(picks, x, dims):
    both = mxu(picks, jnp.concatenate(split(x), axis=1), dims)
    return both[:, :x.shape[1]] + both[:, x.shape[1]:]


def iota(shape, dim):
    return lax.broadcasted_iota(jnp.int32, shape, dim)


def turn(x, shift, axis):
    return pltpu.roll(x, shift % x.shape[axis], axis)


def kernel(
    n, tests, wells, *refs
):
    inputs = refs[:10]
    grad_ref, pred_ref = refs[10:12]
    held = refs[12:22]
    local_sem = refs[22]
    run(
        n, tests, wells, inputs, local_sem, *held, grad_ref, pred_ref, *refs[23:]
    )


def run(
    n, tests, wells, inputs, local_sem, rates_s, test_s,
    logc_ref, store_ref, rech_ref, obs_ref, tile_ref, row_ref, col_ref, screen_ref,
    grad_ref, pred_ref,
    halo, info, picks, near, coef, heads_ref, bounds, part, beside, inner, outer, obs_pad,
    halo_send, halo_recv, hl_send, hl_recv, in_send, in_recv, out_send, out_recv,
    side_send, side_recv,
):
    layers, strip, columns = logc_ref.shape
    assert layers == 2
    rows = 3 * strip
    both = layers * rows
    wide = info.shape[1]
    wpad = near.shape[0]
    packed = near.shape[1]
    lanes = columns + packed
    me = lax.axis_index("tile")
    held = (
        rates_s, test_s, logc_ref, store_ref, rech_ref, obs_ref, tile_ref, row_ref, col_ref,
        screen_ref,
    )
    fetches = [
        pltpu.make_async_copy(src, dst, local_sem.at[index])
        for index, (src, dst) in enumerate(zip(inputs, held))
    ]

    wide_in = inner_size(n)
    wide_out = n // wide_in
    place_in, place_out = lax.rem(me, wide_in), me // wide_in

    def inner_peer(k):
        return place_out * wide_in + lax.rem(place_in + k, wide_in)

    def outer_peer(k):
        return lax.rem(place_out + k, wide_out) * wide_in + place_in

    def remote(src, dst, send_sem, recv_sem, target):
        return pltpu.make_async_remote_copy(
            src_ref=src, dst_ref=dst, send_sem=send_sem, recv_sem=recv_sem,
            device_id={"tile": target}, device_id_type=pl.DeviceIdType.MESH,
        )

    sides = ((0, me < n - 1, me > 0, me + 1), (1, me > 0, me < n - 1, me - 1))
    barrier = pltpu.get_barrier_semaphore()

    def greet(target):
        pl.semaphore_signal(
            barrier, inc=1, device_id={"tile": target}, device_id_type=pl.DeviceIdType.MESH
        )

    next_outside = (place_in == wide_in - 1) & (me < n - 1)
    last_outside = (place_in == 0) & (me > 0)

    @pl.when(next_outside)
    def _():
        greet(me + 1)

    @pl.when(last_outside)
    def _():
        greet(me - 1)

    for k in range(1, wide_in):
        greet(inner_peer(k))
    for k in range(1, wide_out):
        greet(outer_peer(k))
    for fetch in fetches:
        fetch.start()
    outside = next_outside.astype(jnp.int32) + last_outside.astype(jnp.int32)
    pl.semaphore_wait(barrier, wide_in + wide_out - 2 + outside)
    def halo_copy(side, index):
        return remote(
            inputs[2 + index], halo.at[side, index], halo_send.at[side, index],
            halo_recv.at[side, index], sides[side][3],
        )

    fills = (-1e30, 0.0, 0.0)
    for index in range(3):
        for side, sends, gets, target in sides:
            @pl.when(sends)
            def _():
                halo_copy(side, index).start()

    for side, sends, gets, target in sides:
        @pl.when(jnp.logical_not(gets))
        def _():
            for index in range(3):
                halo[side, index] = jnp.full((layers, strip, columns), fills[index], F32)
            beside[side] = jnp.zeros(part.shape, F32)

    for fetch in fetches:
        fetch.wait()

    info[...] = jnp.full(info.shape, -4000.0, F32)
    info[0:1, 0:wells] = col_ref[...].astype(F32)
    info[1:2, 0:wells] = ((tile_ref[...] - me) * strip + row_ref[...] + strip).astype(F32)
    info[2:4, 0:wells] = screen_ref[...].astype(F32)
    well_col = info[0:1, 0:wpad]
    well_row = info[1:2, 0:wpad]
    top = info[2:3, 0:wpad]
    bottom = info[3:4, 0:wpad]
    length = jnp.where(bottom > top, bottom - top, 1.0)
    screens = [
        jnp.where((top <= layer) & (bottom > layer), 1.0 / length, 0.0) for layer in range(layers)
    ]
    trow = iota((16, 1), 0)
    pumped = jnp.full((16, 1), -1, jnp.int32)
    rate = jnp.zeros((16, 1), F32)
    for t in range(tests):
        pumped = jnp.where(trow == t, test_s[t], pumped)
        rate = jnp.where(trow == t, rates_s[t], rate)
    chosen = iota((16, wpad), 1) == pumped

    def at_pumped(values):
        return jnp.sum(jnp.where(chosen, values, 0.0), axis=1, keepdims=True)

    slot = iota((16, packed), 1) - WINDOW * trow
    segment = (slot >= 0) & (slot < WINDOW) & (trow < tests)

    def to_lanes(column):
        return jnp.sum(jnp.where(segment, column, 0.0), axis=0, keepdims=True)

    label = jnp.sum(
        jnp.where(segment, at_pumped(well_col) - HALF + slot.astype(F32), 0.0),
        axis=0, keepdims=True,
    )
    label = jnp.where(iota((1, packed), 1) < tests * WINDOW, label, -2000.0)
    info[0:1, wpad:] = label
    pump_row = to_lanes(at_pumped(well_row))
    centre = segment & (slot == HALF)
    amounts = [
        jnp.sum(jnp.where(centre, -rate * at_pumped(screen), 0.0), axis=0, keepdims=True)
        for screen in screens
    ]
    line = iota((rows, 1), 0).astype(F32)
    pumping = jnp.concatenate(
        [jnp.where(line == pump_row, amount, 0.0) for amount in amounts], axis=0
    )
    rowsel = jnp.concatenate(
        [jnp.where(line == well_row, screen, 0.0) for screen in screens], axis=0
    )
    upright = info[...].T[:, 0:1]
    picks[...] = jnp.where(
        upright == iota((wide, columns), 1).astype(F32), 1.0, 0.0
    ).astype(BF16)
    near[...] = jnp.where(upright[0:wpad] == label, 1.0, 0.0)
    obs_pad[...] = jnp.zeros(obs_pad.shape, F32)
    obs_pad[0:tests, 0:wells] = obs_ref[...]

    def await_halo(indices):
        for side, sends, gets, target in sides:
            @pl.when(gets)
            def _():
                for index in indices:
                    halo_copy(side, index).wait_recv()

    await_halo((0,))

    def extended(ref, index):
        return jnp.concatenate(
            [
                piece
                for layer in range(layers)
                for piece in (halo[0, index, layer], ref[layer], halo[1, index, layer])
            ],
            axis=0,
        )

    cond = jnp.exp(extended(logc_ref, 0))
    line2 = lax.rem(iota((both, 1), 0), rows)
    whole_row = line2 + (me - 1) * strip
    linked = (line2 >= 1) & (whole_row >= 1) & (whole_row < n * strip)
    column = iota((1, columns), 1)
    face_up = 0.5 * (cond + turn(cond, 1, 0))
    up = jnp.where(linked, face_up, 0.0)
    left_open = 0.5 * (cond + turn(cond, 1, 1))
    left = jnp.where(column == 0, 0.0, left_open)
    face_left = jnp.where(column == 0, 0.5 * cond, left_open)
    face_right = jnp.where(column == columns - 1, 0.5 * cond, turn(left_open, -1, 1))
    across = 0.5 * (cond + turn(cond, rows, 0))
    faces = face_up + turn(face_up, -1, 0) + face_left + face_right + across

    def own(x):
        return jnp.concatenate(
            [x[layer * rows + strip:layer * rows + 2 * strip] for layer in range(layers)], axis=0
        )

    store_own = jnp.concatenate([store_ref[layer] for layer in range(layers)], axis=0)
    high_own = jnp.max(store_own + 2.0 * own(faces), keepdims=True)
    low_own = jnp.min(store_own, keepdims=True)
    bounds[0] = jnp.where(iota((1, 128), 1) < 64, high_own, -low_own)

    def bound_in(k):
        return remote(bounds.at[0], bounds.at[k], hl_send.at[k], hl_recv.at[k], inner_peer(k))

    def bound_out(k):
        at = wide_in + k
        return remote(
            bounds.at[wide_in], bounds.at[at], hl_send.at[at], hl_recv.at[at], outer_peer(k)
        )

    for k in range(1, wide_in):
        bound_in(k).start()
    await_halo((1, 2))
    store = extended(store_ref, 1)
    diag = store + faces

    stacked = jnp.concatenate([diag, up, left, across], axis=0)
    taken = exact_left(stacked, picks[wpad:, :], NT)
    for index, whole in enumerate((diag, up, left, across)):
        coef[index, :, 0:columns] = whole
        coef[index, :, columns:] = taken[index * both:(index + 1) * both]
    coef[2, :, columns:columns + 128] = jnp.where(
        iota((1, 128), 1) == 0, 0.0, taken[2 * both:3 * both, 0:128]
    )

    def operate(v):
        out = coef[0] * v - coef[1] * turn(v, 1, 0) - turn(coef[1] * v, -1, 0)
        out = out - coef[2] * turn(v, 1, 1) - turn(coef[2] * v, -1, 1)
        return out - coef[3] * turn(v, rows, 0)

    for k in range(1, wide_in):
        bound_in(k).wait_recv()
    bounds[wide_in] = jnp.max(bounds[0:wide_in], axis=0)
    for k in range(1, wide_out):
        bound_out(k).start()
    source = jnp.concatenate([extended(rech_ref, 2), pumping], axis=1)
    applied = operate(source)
    for k in range(1, wide_out):
        bound_out(k).wait_recv()
    bound = jnp.max(bounds[wide_in:], axis=0)
    high = bound[:, 0:1]
    low = -bound[:, 64:65]
    center = 0.5 * (high + low)
    radius = 0.5 * (high - low)
    spread = center / radius

    def chebyshev(source, applied):
        ratio = 1.0 / spread
        direction = source / center
        iterate = direction
        residual = source
        for step in range(ITERS):
            if step == 0:
                residual = residual - applied / center
            else:
                residual = residual - operate(direction)
            following = 1.0 / (2.0 * spread - ratio)
            direction = (following * ratio) * direction + (2.0 * following / radius) * residual
            iterate = iterate + direction
            ratio = following
        return iterate

    heads = chebyshev(source, applied)
    heads_ref[...] = heads
    mine = own(heads)
    rowsel_own = own(rowsel)
    common = jnp.sum(
        exact_left(mine[:, 0:columns], picks[0:wpad, :], NT) * rowsel_own, axis=0, keepdims=True
    )
    deltas = mine[:, columns:]
    place = iota((1, packed), 1)
    spaced = jnp.concatenate(
        [
            jnp.where((place >= t * WINDOW) & (place < (t + 1) * WINDOW), deltas, 0.0)
            for t in range(tests)
        ],
        axis=0,
    )
    read = exact_left(spaced, near[...].astype(BF16), NT)
    depth = layers * strip
    sampled = [
        jnp.sum(read[t * depth:(t + 1) * depth] * rowsel_own, axis=0, keepdims=True) + common
        for t in range(tests)
    ]
    sampled = jnp.concatenate(sampled + [jnp.zeros((16 - tests, wpad), F32)], axis=0)
    banks = wpad // 128
    for k in range(part.shape[0]):
        r, c = 4 * (k // banks), 128 * (k % banks)
        part[k] = sampled[r:r + 4, c:c + 128]

    def side_copy(side):
        return remote(
            part, beside.at[side], side_send.at[side], side_recv.at[side], sides[side][3]
        )

    def part_in(k):
        return remote(part, inner.at[k], in_send.at[k], in_recv.at[k], inner_peer(k))

    def part_out(k):
        return remote(inner.at[0], outer.at[k], out_send.at[k], out_recv.at[k], outer_peer(k))

    for side, sends, gets, target in sides:
        @pl.when(sends)
        def _():
            side_copy(side).start()

    for k in range(1, wide_in):
        part_in(k).start()
    for k in range(1, wide_in):
        part_in(k).wait_recv()
    mixed = part[...]
    for k in range(1, wide_in):
        mixed = mixed + inner[k]
    inner[0] = mixed
    for k in range(1, wide_out):
        part_out(k).start()
    for side, sends, gets, target in sides:
        @pl.when(gets)
        def _():
            side_copy(side).wait_recv()

    def assembled(x):
        bands = [
            jnp.concatenate([x[r * banks + c] for c in range(banks)], axis=1)
            for r in range(part.shape[0] // banks)
        ]
        empty = 16 - 4 * len(bands)
        return jnp.concatenate(bands + ([jnp.zeros((empty, wpad), F32)] if empty else []), axis=0)

    valid = (iota((16, wpad), 0) < tests) & (iota((16, wpad), 1) < wells)
    misfit = assembled(part[...] + beside[0] + beside[1]) - obs_pad[...]
    misfit = jnp.where(valid, misfit, 0.0)

    summed = jnp.sum(misfit, axis=0, keepdims=True)
    dense = exact_left(rowsel * summed, picks[0:wpad, :], NN)
    segment_f = jnp.where(segment, 1.0, 0.0).astype(BF16)
    spread_weight = mxu(
        jnp.concatenate(split(misfit), axis=0),
        jnp.concatenate([segment_f, segment_f], axis=0), TN,
    )
    placed = exact_right(rowsel.astype(BF16), spread_weight * near[...], NN)
    source = jnp.concatenate([dense, placed], axis=1)
    adjoint = chebyshev(source, operate(source))

    heads = heads_ref[...]
    lane = iota((1, lanes), 1)
    start = (lane == 0) | (lane == columns)

    def before(x):
        return jnp.where(start, 0.0, turn(x, 1, 1))

    term_x = 0.5 * (adjoint - turn(adjoint, 1, 0)) * (heads - turn(heads, 1, 0))
    x_sum = term_x + turn(term_x, -1, 0)
    term_y = 0.5 * (adjoint - before(adjoint)) * (heads - before(heads))
    term_right = jnp.where(
        lane == columns - 1, 0.5 * adjoint * heads, turn(term_y, -1, 1)
    )
    term_z = 0.5 * (adjoint - turn(adjoint, rows, 0)) * (heads - turn(heads, rows, 0))
    cells = own(x_sum + term_y + term_right + term_z)
    cells = cells[:, 0:columns] + exact_left(cells[:, columns:], picks[wpad:, :], NN)
    for k in range(1, wide_out):
        part_out(k).wait_recv()
    total = inner[0]
    for k in range(1, wide_out):
        total = total + outer[k]
    predicted = assembled(total)
    pred_ref[...] = predicted[0:tests, 0:wells]
    misfit = jnp.where(valid, predicted - obs_pad[...], 0.0)
    square = jnp.sum(misfit * misfit, keepdims=True)
    gain = -1.0 / jnp.sqrt(square / (tests * wells) + 1e-06)
    for layer in range(layers):
        grad_ref[layer] = jnp.exp(logc_ref[layer]) * (
            gain * cells[layer * strip:(layer + 1) * strip]
        )

    for side, sends, gets, target in sides:
        @pl.when(sends)
        def _():
            for index in range(3):
                halo_copy(side, index).wait_send()
            side_copy(side).wait_send()

    for k in range(1, wide_in):
        bound_in(k).wait_send()
        part_in(k).wait_send()
    for k in range(1, wide_out):
        bound_out(k).wait_send()
        part_out(k).wait_send()


def inner_size(n):
    size = 1
    while 4 * size * size <= n and n % (2 * size) == 0:
        size *= 2
    return size


def round_up(value, unit):
    return -(-value // unit) * unit


def local(
    log_conductivity, storage, recharge, observed, rates,
    well_tile, well_row, well_col, well_screen, test_well,
):
    layers, strip, columns = log_conductivity.shape
    tests, wells = observed.shape
    n = lax.axis_size("tile")
    wpad = round_up(wells, 128)
    packed = round_up(tests * WINDOW, 128)
    both = layers * 3 * strip
    lanes = columns + packed
    slots = round_up(tests, 4) // 4 * (wpad // 128)
    wide_in = inner_size(n)
    wide_out = n // wide_in
    vmem = pl.BlockSpec(memory_space=pltpu.VMEM)
    dma = pltpu.SemaphoreType.DMA
    return pl.pallas_call(
        functools.partial(kernel, n, tests, wells),
        out_shape=(
            jax.ShapeDtypeStruct((layers, strip, columns), F32),
            jax.ShapeDtypeStruct((tests, wells), F32),
        ),
        in_specs=[pl.BlockSpec(memory_space=pl.ANY)] * 10,
        out_specs=(vmem, vmem),
        scratch_shapes=[
            pltpu.SMEM((tests,), F32),
            pltpu.SMEM((tests,), jnp.int32),
            pltpu.VMEM((layers, strip, columns), F32),
            pltpu.VMEM((layers, strip, columns), F32),
            pltpu.VMEM((layers, strip, columns), F32),
            pltpu.VMEM((tests, wells), F32),
            pltpu.VMEM((1, wells), jnp.int32),
            pltpu.VMEM((1, wells), jnp.int32),
            pltpu.VMEM((1, wells), jnp.int32),
            pltpu.VMEM((2, wells), jnp.int32),
            dma((10,)),
            pltpu.VMEM((2, 3, layers, strip, columns), F32),
            pltpu.VMEM((8, wpad + packed), F32),
            pltpu.VMEM((wpad + packed, columns), BF16),
            pltpu.VMEM((wpad, packed), F32),
            pltpu.VMEM((4, both, lanes), F32),
            pltpu.VMEM((both, lanes), F32),
            pltpu.VMEM((wide_in + wide_out, 1, 128), F32),
            pltpu.VMEM((slots, 4, 128), F32),
            pltpu.VMEM((2, slots, 4, 128), F32),
            pltpu.VMEM((wide_in, slots, 4, 128), F32),
            pltpu.VMEM((wide_out, slots, 4, 128), F32),
            pltpu.VMEM((16, wpad), F32),
            dma((2, 3)), dma((2, 3)), dma((wide_in + wide_out,)), dma((wide_in + wide_out,)),
            dma((wide_in,)), dma((wide_in,)), dma((wide_out,)), dma((wide_out,)),
            dma((2,)), dma((2,)),
        ],
        compiler_params=pltpu.CompilerParams(
            collective_id=0, has_side_effects=True, vmem_limit_bytes=56 * 1024 * 1024
        ),
    )(
        rates, test_well, log_conductivity, storage, recharge, observed,
        well_tile.reshape(1, wells), well_row.reshape(1, wells), well_col.reshape(1, wells),
        well_screen.T,
    )


def solution(mesh):
    return jax.shard_map(
        local,
        mesh=mesh,
        in_specs=(
            P("groups", "tile", None),
            P("groups", "tile", None),
            P("groups", "tile", None),
            P("groups", None),
            P("groups"),
            P(),
            P(),
            P(),
            P(),
            P(),
        ),
        out_specs=(P("groups", "tile", None), P("groups", None)),
        check_vma=False,
    )
```

```python
import functools

import jax
import jax.numpy as jnp
from jax import lax
from jax.experimental import pallas as pl
from jax.experimental.pallas import tpu as pltpu
from jax.sharding import PartitionSpec as P

ITERS = 4
HALF = 2 * ITERS + 2
WINDOW = 2 * HALF + 1
F32 = jnp.float32
BF16 = jnp.bfloat16
NT = (((1,), (1,)), ((), ()))
NN = (((1,), (0,)), ((), ()))
TN = (((0,), (0,)), ((), ()))


def split(x):
    high = x.astype(BF16)
    return high, (x - high.astype(F32)).astype(BF16)


def mxu(a, b, dims):
    return lax.dot_general(a, b, dims, preferred_element_type=F32)


def exact_left(x, picks, dims):
    both = mxu(jnp.concatenate(split(x), axis=0), picks, dims)
    return both[:x.shape[0]] + both[x.shape[0]:]


def exact_right(picks, x, dims):
    both = mxu(picks, jnp.concatenate(split(x), axis=1), dims)
    return both[:, :x.shape[1]] + both[:, x.shape[1]:]


def iota(shape, dim):
    return lax.broadcasted_iota(jnp.int32, shape, dim)


def turn(x, shift, axis):
    return pltpu.roll(x, shift % x.shape[axis], axis)


def kernel(
    n, tests, wells, *refs
):
    inputs = refs[:10]
    grad_ref, pred_ref = refs[10:12]
    held = refs[12:22]
    local_sem = refs[22]
    run(
        n, tests, wells, inputs, local_sem, *held, grad_ref, pred_ref, *refs[23:]
    )


def run(
    n, tests, wells, inputs, local_sem, rates_s, test_s,
    logc_ref, store_ref, rech_ref, obs_ref, tile_ref, row_ref, col_ref, screen_ref,
    grad_ref, pred_ref,
    halo, info, picks, near, coef, heads_ref, bounds, part, beside, inner, outer, obs_pad,
    halo_send, halo_recv, hl_send, hl_recv, in_send, in_recv, out_send, out_recv,
    side_send, side_recv,
):
    layers, strip, columns = logc_ref.shape
    assert layers == 2
    rows = 3 * strip
    both = layers * rows
    wide = info.shape[1]
    wpad = near.shape[0]
    packed = near.shape[1]
    lanes = columns + packed
    me = lax.axis_index("tile")
    held = (
        rates_s, test_s, logc_ref, store_ref, rech_ref, obs_ref, tile_ref, row_ref, col_ref,
        screen_ref,
    )
    fetches = [
        pltpu.make_async_copy(src, dst, local_sem.at[index])
        for index, (src, dst) in enumerate(zip(inputs, held))
    ]

    wide_in = inner_size(n)
    wide_out = n // wide_in
    place_in, place_out = lax.rem(me, wide_in), me // wide_in

    def inner_peer(k):
        return place_out * wide_in + lax.rem(place_in + k, wide_in)

    def outer_peer(k):
        return lax.rem(place_out + k, wide_out) * wide_in + place_in

    def remote(src, dst, send_sem, recv_sem, target):
        return pltpu.make_async_remote_copy(
            src_ref=src, dst_ref=dst, send_sem=send_sem, recv_sem=recv_sem,
            device_id={"tile": target}, device_id_type=pl.DeviceIdType.MESH,
        )

    sides = ((0, me < n - 1, me > 0, me + 1), (1, me > 0, me < n - 1, me - 1))
    barrier = pltpu.get_barrier_semaphore()

    def greet(target):
        pl.semaphore_signal(
            barrier, inc=1, device_id={"tile": target}, device_id_type=pl.DeviceIdType.MESH
        )

    next_outside = (place_in == wide_in - 1) & (me < n - 1)
    last_outside = (place_in == 0) & (me > 0)

    @pl.when(next_outside)
    def _():
        greet(me + 1)

    @pl.when(last_outside)
    def _():
        greet(me - 1)

    for k in range(1, wide_in):
        greet(inner_peer(k))
    for k in range(1, wide_out):
        greet(outer_peer(k))
    for fetch in fetches:
        fetch.start()
    outside = next_outside.astype(jnp.int32) + last_outside.astype(jnp.int32)
    pl.semaphore_wait(barrier, wide_in + wide_out - 2 + outside)
    reach = min(strip, ITERS + 1)

    def halo_copy(side, index):
        rows_sent = pl.ds(strip - reach, reach) if side == 0 else pl.ds(0, reach)
        return remote(
            inputs[2 + index].at[:, rows_sent], halo.at[side, index, :, rows_sent], halo_send.at[side, index],
            halo_recv.at[side, index], sides[side][3],
        )

    fills = (-1e30, 0.0, 0.0)
    for index in range(3):
        for side, sends, gets, target in sides:
            @pl.when(sends)
            def _():
                halo_copy(side, index).start()

    for side, sends, gets, target in sides:
        @pl.when(jnp.logical_not(gets))
        def _():
            for index in range(3):
                halo[side, index] = jnp.full((layers, strip, columns), fills[index], F32)
            beside[side] = jnp.zeros(part.shape, F32)

    for fetch in fetches:
        fetch.wait()

    info[...] = jnp.full(info.shape, -4000.0, F32)
    info[0:1, 0:wells] = col_ref[...].astype(F32)
    info[1:2, 0:wells] = ((tile_ref[...] - me) * strip + row_ref[...] + strip).astype(F32)
    info[2:4, 0:wells] = screen_ref[...].astype(F32)
    well_col = info[0:1, 0:wpad]
    well_row = info[1:2, 0:wpad]
    top = info[2:3, 0:wpad]
    bottom = info[3:4, 0:wpad]
    length = jnp.where(bottom > top, bottom - top, 1.0)
    screens = [
        jnp.where((top <= layer) & (bottom > layer), 1.0 / length, 0.0) for layer in range(layers)
    ]
    trow = iota((16, 1), 0)
    pumped = jnp.full((16, 1), -1, jnp.int32)
    rate = jnp.zeros((16, 1), F32)
    for t in range(tests):
        pumped = jnp.where(trow == t, test_s[t], pumped)
        rate = jnp.where(trow == t, rates_s[t], rate)
    chosen = iota((16, wpad), 1) == pumped

    def at_pumped(values):
        return jnp.sum(jnp.where(chosen, values, 0.0), axis=1, keepdims=True)

    slot = iota((16, packed), 1) - WINDOW * trow
    segment = (slot >= 0) & (slot < WINDOW) & (trow < tests)

    def to_lanes(column):
        return jnp.sum(jnp.where(segment, column, 0.0), axis=0, keepdims=True)

    label = jnp.sum(
        jnp.where(segment, at_pumped(well_col) - HALF + slot.astype(F32), 0.0),
        axis=0, keepdims=True,
    )
    label = jnp.where(iota((1, packed), 1) < tests * WINDOW, label, -2000.0)
    info[0:1, wpad:] = label
    pump_row = to_lanes(at_pumped(well_row))
    centre = segment & (slot == HALF)
    amounts = [
        jnp.sum(jnp.where(centre, -rate * at_pumped(screen), 0.0), axis=0, keepdims=True)
        for screen in screens
    ]
    line = iota((rows, 1), 0).astype(F32)
    pumping = jnp.concatenate(
        [jnp.where(line == pump_row, amount, 0.0) for amount in amounts], axis=0
    )
    rowsel = jnp.concatenate(
        [jnp.where(line == well_row, screen, 0.0) for screen in screens], axis=0
    )
    upright = info[...].T[:, 0:1]
    picks[...] = jnp.where(
        upright == iota((wide, columns), 1).astype(F32), 1.0, 0.0
    ).astype(BF16)
    near[...] = jnp.where(upright[0:wpad] == label, 1.0, 0.0)
    obs_pad[...] = jnp.zeros(obs_pad.shape, F32)
    obs_pad[0:tests, 0:wells] = obs_ref[...]

    def await_halo(indices):
        for side, sends, gets, target in sides:
            @pl.when(gets)
            def _():
                for index in indices:
                    halo_copy(side, index).wait_recv()

    await_halo((0,))

    def extended(ref, index):
        return jnp.concatenate(
            [
                piece
                for layer in range(layers)
                for piece in (halo[0, index, layer], ref[layer], halo[1, index, layer])
            ],
            axis=0,
        )

    cond = jnp.exp(extended(logc_ref, 0))
    line2 = lax.rem(iota((both, 1), 0), rows)
    whole_row = line2 + (me - 1) * strip
    linked = (line2 >= 1) & (whole_row >= 1) & (whole_row < n * strip)
    column = iota((1, columns), 1)
    face_up = 0.5 * (cond + turn(cond, 1, 0))
    up = jnp.where(linked, face_up, 0.0)
    left_open = 0.5 * (cond + turn(cond, 1, 1))
    left = jnp.where(column == 0, 0.0, left_open)
    face_left = jnp.where(column == 0, 0.5 * cond, left_open)
    face_right = jnp.where(column == columns - 1, 0.5 * cond, turn(left_open, -1, 1))
    across = 0.5 * (cond + turn(cond, rows, 0))
    faces = face_up + turn(face_up, -1, 0) + face_left + face_right + across

    def own(x):
        return jnp.concatenate(
            [x[layer * rows + strip:layer * rows + 2 * strip] for layer in range(layers)], axis=0
        )

    store_own = jnp.concatenate([store_ref[layer] for layer in range(layers)], axis=0)
    high_own = jnp.max(store_own + 2.0 * own(faces), keepdims=True)
    low_own = jnp.min(store_own, keepdims=True)
    bounds[0] = jnp.where(iota((1, 128), 1) < 64, high_own, -low_own)

    def bound_in(k):
        return remote(bounds.at[0], bounds.at[k], hl_send.at[k], hl_recv.at[k], inner_peer(k))

    def bound_out(k):
        at = wide_in + k
        return remote(
            bounds.at[wide_in], bounds.at[at], hl_send.at[at], hl_recv.at[at], outer_peer(k)
        )

    for k in range(1, wide_in):
        bound_in(k).start()
    await_halo((1, 2))
    store = extended(store_ref, 1)
    diag = store + faces

    stacked = jnp.concatenate([diag, up, left, across], axis=0)
    taken = exact_left(stacked, picks[wpad:, :], NT)
    for index, whole in enumerate((diag, up, left, across)):
        coef[index, :, 0:columns] = whole
        coef[index, :, columns:] = taken[index * both:(index + 1) * both]
    coef[2, :, columns:columns + 128] = jnp.where(
        iota((1, 128), 1) == 0, 0.0, taken[2 * both:3 * both, 0:128]
    )

    def operate(v):
        out = coef[0] * v - coef[1] * turn(v, 1, 0) - turn(coef[1] * v, -1, 0)
        out = out - coef[2] * turn(v, 1, 1) - turn(coef[2] * v, -1, 1)
        return out - coef[3] * turn(v, rows, 0)

    for k in range(1, wide_in):
        bound_in(k).wait_recv()
    bounds[wide_in] = jnp.max(bounds[0:wide_in], axis=0)
    for k in range(1, wide_out):
        bound_out(k).start()
    source = jnp.concatenate([extended(rech_ref, 2), pumping], axis=1)
    applied = operate(source)
    for k in range(1, wide_out):
        bound_out(k).wait_recv()
    bound = jnp.max(bounds[wide_in:], axis=0)
    high = bound[:, 0:1]
    low = -bound[:, 64:65]
    center = 0.5 * (high + low)
    radius = 0.5 * (high - low)
    spread = center / radius

    def chebyshev(source, applied):
        ratio = 1.0 / spread
        direction = source / center
        iterate = direction
        residual = source
        for step in range(ITERS):
            if step == 0:
                residual = residual - applied / center
            else:
                residual = residual - operate(direction)
            following = 1.0 / (2.0 * spread - ratio)
            direction = (following * ratio) * direction + (2.0 * following / radius) * residual
            iterate = iterate + direction
            ratio = following
        return iterate

    heads = chebyshev(source, applied)
    heads_ref[...] = heads
    mine = own(heads)
    rowsel_own = own(rowsel)
    common = jnp.sum(
        exact_left(mine[:, 0:columns], picks[0:wpad, :], NT) * rowsel_own, axis=0, keepdims=True
    )
    deltas = mine[:, columns:]
    place = iota((1, packed), 1)
    spaced = jnp.concatenate(
        [
            jnp.where((place >= t * WINDOW) & (place < (t + 1) * WINDOW), deltas, 0.0)
            for t in range(tests)
        ],
        axis=0,
    )
    read = exact_left(spaced, near[...].astype(BF16), NT)
    depth = layers * strip
    sampled = [
        jnp.sum(read[t * depth:(t + 1) * depth] * rowsel_own, axis=0, keepdims=True) + common
        for t in range(tests)
    ]
    sampled = jnp.concatenate(sampled + [jnp.zeros((16 - tests, wpad), F32)], axis=0)
    banks = wpad // 128
    for k in range(part.shape[0]):
        r, c = 4 * (k // banks), 128 * (k % banks)
        part[k] = sampled[r:r + 4, c:c + 128]

    def side_copy(side):
        return remote(
            part, beside.at[side], side_send.at[side], side_recv.at[side], sides[side][3]
        )

    def part_in(k):
        return remote(part, inner.at[k], in_send.at[k], in_recv.at[k], inner_peer(k))

    def part_out(k):
        return remote(inner.at[0], outer.at[k], out_send.at[k], out_recv.at[k], outer_peer(k))

    for side, sends, gets, target in sides:
        @pl.when(sends)
        def _():
            side_copy(side).start()

    for k in range(1, wide_in):
        part_in(k).start()
    for k in range(1, wide_in):
        part_in(k).wait_recv()
    mixed = part[...]
    for k in range(1, wide_in):
        mixed = mixed + inner[k]
    inner[0] = mixed
    for k in range(1, wide_out):
        part_out(k).start()
    for side, sends, gets, target in sides:
        @pl.when(gets)
        def _():
            side_copy(side).wait_recv()

    def assembled(x):
        bands = [
            jnp.concatenate([x[r * banks + c] for c in range(banks)], axis=1)
            for r in range(part.shape[0] // banks)
        ]
        empty = 16 - 4 * len(bands)
        return jnp.concatenate(bands + ([jnp.zeros((empty, wpad), F32)] if empty else []), axis=0)

    valid = (iota((16, wpad), 0) < tests) & (iota((16, wpad), 1) < wells)
    misfit = assembled(part[...] + beside[0] + beside[1]) - obs_pad[...]
    misfit = jnp.where(valid, misfit, 0.0)

    summed = jnp.sum(misfit, axis=0, keepdims=True)
    dense = exact_left(rowsel * summed, picks[0:wpad, :], NN)
    segment_f = jnp.where(segment, 1.0, 0.0).astype(BF16)
    spread_weight = mxu(
        jnp.concatenate(split(misfit), axis=0),
        jnp.concatenate([segment_f, segment_f], axis=0), TN,
    )
    placed = exact_right(rowsel.astype(BF16), spread_weight * near[...], NN)
    source = jnp.concatenate([dense, placed], axis=1)
    adjoint = chebyshev(source, operate(source))

    heads = heads_ref[...]
    lane = iota((1, lanes), 1)
    start = (lane == 0) | (lane == columns)

    def before(x):
        return jnp.where(start, 0.0, turn(x, 1, 1))

    term_x = 0.5 * (adjoint - turn(adjoint, 1, 0)) * (heads - turn(heads, 1, 0))
    x_sum = term_x + turn(term_x, -1, 0)
    term_y = 0.5 * (adjoint - before(adjoint)) * (heads - before(heads))
    term_right = jnp.where(
        lane == columns - 1, 0.5 * adjoint * heads, turn(term_y, -1, 1)
    )
    term_z = 0.5 * (adjoint - turn(adjoint, rows, 0)) * (heads - turn(heads, rows, 0))
    cells = own(x_sum + term_y + term_right + term_z)
    cells = cells[:, 0:columns] + exact_left(cells[:, columns:], picks[wpad:, :], NN)
    for k in range(1, wide_out):
        part_out(k).wait_recv()
    total = inner[0]
    for k in range(1, wide_out):
        total = total + outer[k]
    predicted = assembled(total)
    pred_ref[...] = predicted[0:tests, 0:wells]
    misfit = jnp.where(valid, predicted - obs_pad[...], 0.0)
    square = jnp.sum(misfit * misfit, keepdims=True)
    gain = -1.0 / jnp.sqrt(square / (tests * wells) + 1e-06)
    for layer in range(layers):
        grad_ref[layer] = jnp.exp(logc_ref[layer]) * (
            gain * cells[layer * strip:(layer + 1) * strip]
        )

    for side, sends, gets, target in sides:
        @pl.when(sends)
        def _():
            for index in range(3):
                halo_copy(side, index).wait_send()
            side_copy(side).wait_send()

    for k in range(1, wide_in):
        bound_in(k).wait_send()
        part_in(k).wait_send()
    for k in range(1, wide_out):
        bound_out(k).wait_send()
        part_out(k).wait_send()


def inner_size(n):
    size = 1
    while 4 * size * size <= n and n % (2 * size) == 0:
        size *= 2
    return size


def round_up(value, unit):
    return -(-value // unit) * unit


def local(
    log_conductivity, storage, recharge, observed, rates,
    well_tile, well_row, well_col, well_screen, test_well,
):
    layers, strip, columns = log_conductivity.shape
    tests, wells = observed.shape
    n = lax.axis_size("tile")
    wpad = round_up(wells, 128)
    packed = round_up(tests * WINDOW, 128)
    both = layers * 3 * strip
    lanes = columns + packed
    slots = round_up(tests, 4) // 4 * (wpad // 128)
    wide_in = inner_size(n)
    wide_out = n // wide_in
    vmem = pl.BlockSpec(memory_space=pltpu.VMEM)
    dma = pltpu.SemaphoreType.DMA
    return pl.pallas_call(
        functools.partial(kernel, n, tests, wells),
        out_shape=(
            jax.ShapeDtypeStruct((layers, strip, columns), F32),
            jax.ShapeDtypeStruct((tests, wells), F32),
        ),
        in_specs=[pl.BlockSpec(memory_space=pl.ANY)] * 10,
        out_specs=(vmem, vmem),
        scratch_shapes=[
            pltpu.SMEM((tests,), F32),
            pltpu.SMEM((tests,), jnp.int32),
            pltpu.VMEM((layers, strip, columns), F32),
            pltpu.VMEM((layers, strip, columns), F32),
            pltpu.VMEM((layers, strip, columns), F32),
            pltpu.VMEM((tests, wells), F32),
            pltpu.VMEM((1, wells), jnp.int32),
            pltpu.VMEM((1, wells), jnp.int32),
            pltpu.VMEM((1, wells), jnp.int32),
            pltpu.VMEM((2, wells), jnp.int32),
            dma((10,)),
            pltpu.VMEM((2, 3, layers, strip, columns), F32),
            pltpu.VMEM((8, wpad + packed), F32),
            pltpu.VMEM((wpad + packed, columns), BF16),
            pltpu.VMEM((wpad, packed), F32),
            pltpu.VMEM((4, both, lanes), F32),
            pltpu.VMEM((both, lanes), F32),
            pltpu.VMEM((wide_in + wide_out, 1, 128), F32),
            pltpu.VMEM((slots, 4, 128), F32),
            pltpu.VMEM((2, slots, 4, 128), F32),
            pltpu.VMEM((wide_in, slots, 4, 128), F32),
            pltpu.VMEM((wide_out, slots, 4, 128), F32),
            pltpu.VMEM((16, wpad), F32),
            dma((2, 3)), dma((2, 3)), dma((wide_in + wide_out,)), dma((wide_in + wide_out,)),
            dma((wide_in,)), dma((wide_in,)), dma((wide_out,)), dma((wide_out,)),
            dma((2,)), dma((2,)),
        ],
        compiler_params=pltpu.CompilerParams(
            collective_id=0, has_side_effects=True, vmem_limit_bytes=56 * 1024 * 1024
        ),
    )(
        rates, test_well, log_conductivity, storage, recharge, observed,
        well_tile.reshape(1, wells), well_row.reshape(1, wells), well_col.reshape(1, wells),
        well_screen.T,
    )


def solution(mesh):
    return jax.shard_map(
        local,
        mesh=mesh,
        in_specs=(
            P("groups", "tile", None),
            P("groups", "tile", None),
            P("groups", "tile", None),
            P("groups", None),
            P("groups"),
            P(),
            P(),
            P(),
            P(),
            P(),
        ),
        out_specs=(P("groups", "tile", None), P("groups", None)),
        check_vma=False,
    )
```

```python
import functools

import jax
import jax.numpy as jnp
from jax import lax
from jax.experimental import pallas as pl
from jax.experimental.pallas import tpu as pltpu
from jax.sharding import PartitionSpec as P

ITERS = 4
HALF = 2 * ITERS + 2
WINDOW = 2 * HALF + 1
F32 = jnp.float32
BF16 = jnp.bfloat16
NT = (((1,), (1,)), ((), ()))
NN = (((1,), (0,)), ((), ()))
TN = (((0,), (0,)), ((), ()))


def split(x):
    high = x.astype(BF16)
    return high, (x - high.astype(F32)).astype(BF16)


def mxu(a, b, dims):
    return lax.dot_general(a, b, dims, preferred_element_type=F32)


def exact_left(x, picks, dims):
    both = mxu(jnp.concatenate(split(x), axis=0), picks, dims)
    return both[:x.shape[0]] + both[x.shape[0]:]


def exact_right(picks, x, dims):
    both = mxu(picks, jnp.concatenate(split(x), axis=1), dims)
    return both[:, :x.shape[1]] + both[:, x.shape[1]:]


def iota(shape, dim):
    return lax.broadcasted_iota(jnp.int32, shape, dim)


def turn(x, shift, axis):
    return pltpu.roll(x, shift % x.shape[axis], axis)


def kernel(
    n, tests, wells, *refs
):
    inputs = refs[:10]
    grad_ref, pred_ref = refs[10:12]
    held = refs[12:22]
    local_sem = refs[22]
    run(
        n, tests, wells, inputs, local_sem, *held, grad_ref, pred_ref, *refs[23:]
    )


def run(
    n, tests, wells, inputs, local_sem, rates_s, test_s,
    logc_ref, store_ref, rech_ref, obs_ref, tile_ref, row_ref, col_ref, screen_ref,
    grad_ref, pred_ref,
    halo, info, picks, near, coef, heads_ref, bounds, part, beside, inner, outer, obs_pad,
    halo_send, halo_recv, hl_send, hl_recv, in_send, in_recv, out_send, out_recv,
    side_send, side_recv,
):
    layers, strip, columns = logc_ref.shape
    assert layers == 2
    rows = 3 * strip
    both = layers * rows
    wide = info.shape[1]
    wpad = near.shape[0]
    packed = near.shape[1]
    lanes = columns + packed
    me = lax.axis_index("tile")
    held = (
        rates_s, test_s, logc_ref, store_ref, rech_ref, obs_ref, tile_ref, row_ref, col_ref,
        screen_ref,
    )
    fetches = [
        pltpu.make_async_copy(src, dst, local_sem.at[index])
        for index, (src, dst) in enumerate(zip(inputs, held))
    ]

    wide_in = inner_size(n)
    wide_out = n // wide_in
    place_in, place_out = lax.rem(me, wide_in), me // wide_in

    def inner_peer(k):
        return place_out * wide_in + lax.rem(place_in + k, wide_in)

    def outer_peer(k):
        return lax.rem(place_out + k, wide_out) * wide_in + place_in

    def remote(src, dst, send_sem, recv_sem, target):
        return pltpu.make_async_remote_copy(
            src_ref=src, dst_ref=dst, send_sem=send_sem, recv_sem=recv_sem,
            device_id={"tile": target}, device_id_type=pl.DeviceIdType.MESH,
        )

    sides = ((0, me < n - 1, me > 0, me + 1), (1, me > 0, me < n - 1, me - 1))
    barrier = pltpu.get_barrier_semaphore()

    def greet(target):
        pl.semaphore_signal(
            barrier, inc=1, device_id={"tile": target}, device_id_type=pl.DeviceIdType.MESH
        )

    next_outside = (place_in == wide_in - 1) & (me < n - 1)
    last_outside = (place_in == 0) & (me > 0)

    @pl.when(next_outside)
    def _():
        greet(me + 1)

    @pl.when(last_outside)
    def _():
        greet(me - 1)

    for k in range(1, wide_in):
        greet(inner_peer(k))
    for k in range(1, wide_out):
        greet(outer_peer(k))
    for fetch in fetches:
        fetch.start()
    outside = next_outside.astype(jnp.int32) + last_outside.astype(jnp.int32)
    pl.semaphore_wait(barrier, wide_in + wide_out - 2 + outside)
    reach = min(strip, ITERS + 1)

    def halo_copy(side, index):
        rows_sent = pl.ds(strip - reach, reach) if side == 0 else pl.ds(0, reach)
        return remote(
            inputs[2 + index].at[:, rows_sent], halo.at[side, index, :, rows_sent], halo_send.at[side, index],
            halo_recv.at[side, index], sides[side][3],
        )

    fills = (-1e30, 0.0, 0.0)
    for index in range(3):
        for side, sends, gets, target in sides:
            @pl.when(sends)
            def _():
                halo_copy(side, index).start()

    for side, sends, gets, target in sides:
        @pl.when(jnp.logical_not(gets))
        def _():
            for index in range(3):
                halo[side, index] = jnp.full((layers, strip, columns), fills[index], F32)
            beside[side] = jnp.zeros(part.shape, F32)

    for fetch in fetches:
        fetch.wait()

    info[...] = jnp.full(info.shape, -4000.0, F32)
    info[0:1, 0:wells] = col_ref[...].astype(F32)
    info[1:2, 0:wells] = ((tile_ref[...] - me) * strip + row_ref[...] + strip).astype(F32)
    info[2:4, 0:wells] = screen_ref[...].astype(F32)
    well_col = info[0:1, 0:wpad]
    well_row = info[1:2, 0:wpad]
    top = info[2:3, 0:wpad]
    bottom = info[3:4, 0:wpad]
    length = jnp.where(bottom > top, bottom - top, 1.0)
    screens = [
        jnp.where((top <= layer) & (bottom > layer), 1.0 / length, 0.0) for layer in range(layers)
    ]
    trow = iota((16, 1), 0)
    pumped = jnp.full((16, 1), -1, jnp.int32)
    rate = jnp.zeros((16, 1), F32)
    for t in range(tests):
        pumped = jnp.where(trow == t, test_s[t], pumped)
        rate = jnp.where(trow == t, rates_s[t], rate)
    chosen = iota((16, wpad), 1) == pumped

    def at_pumped(values):
        return jnp.sum(jnp.where(chosen, values, 0.0), axis=1, keepdims=True)

    slot = iota((16, packed), 1) - WINDOW * trow
    segment = (slot >= 0) & (slot < WINDOW) & (trow < tests)

    def to_lanes(column):
        return jnp.sum(jnp.where(segment, column, 0.0), axis=0, keepdims=True)

    label = jnp.sum(
        jnp.where(segment, at_pumped(well_col) - HALF + slot.astype(F32), 0.0),
        axis=0, keepdims=True,
    )
    label = jnp.where(iota((1, packed), 1) < tests * WINDOW, label, -2000.0)
    info[0:1, wpad:] = label
    pump_row = to_lanes(at_pumped(well_row))
    centre = segment & (slot == HALF)
    amounts = [
        jnp.sum(jnp.where(centre, -rate * at_pumped(screen), 0.0), axis=0, keepdims=True)
        for screen in screens
    ]
    line = iota((rows, 1), 0).astype(F32)
    pumping = jnp.concatenate(
        [jnp.where(line == pump_row, amount, 0.0) for amount in amounts], axis=0
    )
    rowsel = jnp.concatenate(
        [jnp.where(line == well_row, screen, 0.0) for screen in screens], axis=0
    )
    upright = info[...].T[:, 0:1]
    picks[...] = jnp.where(
        upright == iota((wide, columns), 1).astype(F32), 1.0, 0.0
    ).astype(BF16)
    near[...] = jnp.where(upright[0:wpad] == label, 1.0, 0.0)
    obs_pad[...] = jnp.zeros(obs_pad.shape, F32)
    obs_pad[0:tests, 0:wells] = obs_ref[...]

    def await_halo(indices):
        for side, sends, gets, target in sides:
            @pl.when(gets)
            def _():
                for index in indices:
                    halo_copy(side, index).wait_recv()

    await_halo((0,))

    def extended(ref, index):
        return jnp.concatenate(
            [
                piece
                for layer in range(layers)
                for piece in (halo[0, index, layer], ref[layer], halo[1, index, layer])
            ],
            axis=0,
        )

    cond = jnp.exp(extended(logc_ref, 0))
    line2 = lax.rem(iota((both, 1), 0), rows)
    whole_row = line2 + (me - 1) * strip
    linked = (line2 >= 1) & (whole_row >= 1) & (whole_row < n * strip)
    column = iota((1, columns), 1)
    face_up = 0.5 * (cond + turn(cond, 1, 0))
    up = jnp.where(linked, face_up, 0.0)
    left_open = 0.5 * (cond + turn(cond, 1, 1))
    left = jnp.where(column == 0, 0.0, left_open)
    face_left = jnp.where(column == 0, 0.5 * cond, left_open)
    face_right = jnp.where(column == columns - 1, 0.5 * cond, turn(left_open, -1, 1))
    across = 0.5 * (cond + turn(cond, rows, 0))
    faces = face_up + turn(face_up, -1, 0) + face_left + face_right + across

    def own(x):
        return jnp.concatenate(
            [x[layer * rows + strip:layer * rows + 2 * strip] for layer in range(layers)], axis=0
        )

    store_own = jnp.concatenate([store_ref[layer] for layer in range(layers)], axis=0)
    high_own = jnp.max(store_own + 2.0 * own(faces), keepdims=True)
    low_own = jnp.min(store_own, keepdims=True)
    bounds[0] = jnp.where(iota((1, 128), 1) < 64, high_own, -low_own)

    def bound_in(k):
        return remote(bounds.at[0], bounds.at[k], hl_send.at[k], hl_recv.at[k], inner_peer(k))

    def bound_out(k):
        at = wide_in + k
        return remote(
            bounds.at[wide_in], bounds.at[at], hl_send.at[at], hl_recv.at[at], outer_peer(k)
        )

    for k in range(1, wide_in):
        bound_in(k).start()
    await_halo((1, 2))
    store = extended(store_ref, 1)
    diag = store + faces

    stacked = jnp.concatenate([diag, up, left, across], axis=0)
    taken = exact_left(stacked, picks[wpad:, :], NT)
    for index, whole in enumerate((diag, up, left, across)):
        coef[index, :, 0:columns] = whole
        coef[index, :, columns:] = taken[index * both:(index + 1) * both]
    coef[2, :, columns:columns + 128] = jnp.where(
        iota((1, 128), 1) == 0, 0.0, taken[2 * both:3 * both, 0:128]
    )

    def operate(v):
        out = coef[0] * v - coef[1] * turn(v, 1, 0) - turn(coef[1] * v, -1, 0)
        out = out - coef[2] * turn(v, 1, 1) - turn(coef[2] * v, -1, 1)
        return out - coef[3] * turn(v, rows, 0)

    source = jnp.concatenate([extended(rech_ref, 2), pumping], axis=1)
    used = (line2 >= strip - ITERS) & (line2 < 2 * strip + ITERS)
    used = used & (whole_row >= 0) & (whole_row < n * strip)
    local_high = jnp.max(jnp.where(used, store + 2.0 * faces, 0.0), keepdims=True)
    local_low = jnp.min(jnp.where(used, store, local_high), keepdims=True)
    shift = 0.5 * (local_high + local_low)
    reduced = 0.5 * (local_high - local_low)
    inverse = 1.0 / reduced

    def scaled(v):
        return (operate(v) - shift * v) * inverse

    powers = [source, scaled(source)]
    for k in range(1, wide_in):
        bound_in(k).wait_recv()
    bounds[wide_in] = jnp.max(bounds[0:wide_in], axis=0)
    for k in range(1, wide_out):
        bound_out(k).start()
    for step in range(1, ITERS):
        powers.append(scaled(powers[-1]))
    for k in range(1, wide_out):
        bound_out(k).wait_recv()
    bound = jnp.max(bounds[wide_in:], axis=0)
    high = bound[:, 0:1]
    low = -bound[:, 64:65]
    center = 0.5 * (high + low)
    radius = 0.5 * (high - low)
    spread = center / radius

    def chebyshev(source, apply):
        ratio = 1.0 / spread
        direction = source / center
        iterate = direction
        residual = source
        for step in range(ITERS):
            residual = residual - apply(direction)
            following = 1.0 / (2.0 * spread - ratio)
            direction = (following * ratio) * direction + (2.0 * following / radius) * residual
            iterate = iterate + direction
            ratio = following
        return iterate

    unit = jnp.where(iota((1, 128), 1) == 0, 1.0, 0.0)
    weights = chebyshev(unit, lambda p: shift * p + reduced * turn(p, 1, 1))
    heads = weights[:, 0:1] * powers[0]
    for k in range(1, ITERS + 1):
        heads = heads + weights[:, k:k + 1] * powers[k]
    heads_ref[...] = heads
    mine = own(heads)
    rowsel_own = own(rowsel)
    common = jnp.sum(
        exact_left(mine[:, 0:columns], picks[0:wpad, :], NT) * rowsel_own, axis=0, keepdims=True
    )
    deltas = mine[:, columns:]
    place = iota((1, packed), 1)
    spaced = jnp.concatenate(
        [
            jnp.where((place >= t * WINDOW) & (place < (t + 1) * WINDOW), deltas, 0.0)
            for t in range(tests)
        ],
        axis=0,
    )
    read = exact_left(spaced, near[...].astype(BF16), NT)
    depth = layers * strip
    sampled = [
        jnp.sum(read[t * depth:(t + 1) * depth] * rowsel_own, axis=0, keepdims=True) + common
        for t in range(tests)
    ]
    sampled = jnp.concatenate(sampled + [jnp.zeros((16 - tests, wpad), F32)], axis=0)
    banks = wpad // 128
    for k in range(part.shape[0]):
        r, c = 4 * (k // banks), 128 * (k % banks)
        part[k] = sampled[r:r + 4, c:c + 128]

    def side_copy(side):
        return remote(
            part, beside.at[side], side_send.at[side], side_recv.at[side], sides[side][3]
        )

    def part_in(k):
        return remote(part, inner.at[k], in_send.at[k], in_recv.at[k], inner_peer(k))

    def part_out(k):
        return remote(inner.at[0], outer.at[k], out_send.at[k], out_recv.at[k], outer_peer(k))

    for side, sends, gets, target in sides:
        @pl.when(sends)
        def _():
            side_copy(side).start()

    for k in range(1, wide_in):
        part_in(k).start()
    for k in range(1, wide_in):
        part_in(k).wait_recv()
    mixed = part[...]
    for k in range(1, wide_in):
        mixed = mixed + inner[k]
    inner[0] = mixed
    for k in range(1, wide_out):
        part_out(k).start()
    for side, sends, gets, target in sides:
        @pl.when(gets)
        def _():
            side_copy(side).wait_recv()

    def assembled(x):
        bands = [
            jnp.concatenate([x[r * banks + c] for c in range(banks)], axis=1)
            for r in range(part.shape[0] // banks)
        ]
        empty = 16 - 4 * len(bands)
        return jnp.concatenate(bands + ([jnp.zeros((empty, wpad), F32)] if empty else []), axis=0)

    valid = (iota((16, wpad), 0) < tests) & (iota((16, wpad), 1) < wells)
    misfit = assembled(part[...] + beside[0] + beside[1]) - obs_pad[...]
    misfit = jnp.where(valid, misfit, 0.0)

    summed = jnp.sum(misfit, axis=0, keepdims=True)
    dense = exact_left(rowsel * summed, picks[0:wpad, :], NN)
    segment_f = jnp.where(segment, 1.0, 0.0).astype(BF16)
    spread_weight = mxu(
        jnp.concatenate(split(misfit), axis=0),
        jnp.concatenate([segment_f, segment_f], axis=0), TN,
    )
    placed = exact_right(rowsel.astype(BF16), spread_weight * near[...], NN)
    source = jnp.concatenate([dense, placed], axis=1)
    adjoint = chebyshev(source, operate)

    heads = heads_ref[...]
    lane = iota((1, lanes), 1)
    start = (lane == 0) | (lane == columns)

    def before(x):
        return jnp.where(start, 0.0, turn(x, 1, 1))

    term_x = 0.5 * (adjoint - turn(adjoint, 1, 0)) * (heads - turn(heads, 1, 0))
    x_sum = term_x + turn(term_x, -1, 0)
    term_y = 0.5 * (adjoint - before(adjoint)) * (heads - before(heads))
    term_right = jnp.where(
        lane == columns - 1, 0.5 * adjoint * heads, turn(term_y, -1, 1)
    )
    term_z = 0.5 * (adjoint - turn(adjoint, rows, 0)) * (heads - turn(heads, rows, 0))
    cells = own(x_sum + term_y + term_right + term_z)
    cells = cells[:, 0:columns] + exact_left(cells[:, columns:], picks[wpad:, :], NN)
    for k in range(1, wide_out):
        part_out(k).wait_recv()
    total = inner[0]
    for k in range(1, wide_out):
        total = total + outer[k]
    predicted = assembled(total)
    pred_ref[...] = predicted[0:tests, 0:wells]
    misfit = jnp.where(valid, predicted - obs_pad[...], 0.0)
    square = jnp.sum(misfit * misfit, keepdims=True)
    gain = -1.0 / jnp.sqrt(square / (tests * wells) + 1e-06)
    for layer in range(layers):
        grad_ref[layer] = jnp.exp(logc_ref[layer]) * (
            gain * cells[layer * strip:(layer + 1) * strip]
        )

    for side, sends, gets, target in sides:
        @pl.when(sends)
        def _():
            for index in range(3):
                halo_copy(side, index).wait_send()
            side_copy(side).wait_send()

    for k in range(1, wide_in):
        bound_in(k).wait_send()
        part_in(k).wait_send()
    for k in range(1, wide_out):
        bound_out(k).wait_send()
        part_out(k).wait_send()


def inner_size(n):
    size = 1
    while 4 * size * size <= n and n % (2 * size) == 0:
        size *= 2
    return size


def round_up(value, unit):
    return -(-value // unit) * unit


def local(
    log_conductivity, storage, recharge, observed, rates,
    well_tile, well_row, well_col, well_screen, test_well,
):
    layers, strip, columns = log_conductivity.shape
    tests, wells = observed.shape
    n = lax.axis_size("tile")
    wpad = round_up(wells, 128)
    packed = round_up(tests * WINDOW, 128)
    both = layers * 3 * strip
    lanes = columns + packed
    slots = round_up(tests, 4) // 4 * (wpad // 128)
    wide_in = inner_size(n)
    wide_out = n // wide_in
    vmem = pl.BlockSpec(memory_space=pltpu.VMEM)
    dma = pltpu.SemaphoreType.DMA
    return pl.pallas_call(
        functools.partial(kernel, n, tests, wells),
        out_shape=(
            jax.ShapeDtypeStruct((layers, strip, columns), F32),
            jax.ShapeDtypeStruct((tests, wells), F32),
        ),
        in_specs=[pl.BlockSpec(memory_space=pl.ANY)] * 10,
        out_specs=(vmem, vmem),
        scratch_shapes=[
            pltpu.SMEM((tests,), F32),
            pltpu.SMEM((tests,), jnp.int32),
            pltpu.VMEM((layers, strip, columns), F32),
            pltpu.VMEM((layers, strip, columns), F32),
            pltpu.VMEM((layers, strip, columns), F32),
            pltpu.VMEM((tests, wells), F32),
            pltpu.VMEM((1, wells), jnp.int32),
            pltpu.VMEM((1, wells), jnp.int32),
            pltpu.VMEM((1, wells), jnp.int32),
            pltpu.VMEM((2, wells), jnp.int32),
            dma((10,)),
            pltpu.VMEM((2, 3, layers, strip, columns), F32),
            pltpu.VMEM((8, wpad + packed), F32),
            pltpu.VMEM((wpad + packed, columns), BF16),
            pltpu.VMEM((wpad, packed), F32),
            pltpu.VMEM((4, both, lanes), F32),
            pltpu.VMEM((both, lanes), F32),
            pltpu.VMEM((wide_in + wide_out, 1, 128), F32),
            pltpu.VMEM((slots, 4, 128), F32),
            pltpu.VMEM((2, slots, 4, 128), F32),
            pltpu.VMEM((wide_in, slots, 4, 128), F32),
            pltpu.VMEM((wide_out, slots, 4, 128), F32),
            pltpu.VMEM((16, wpad), F32),
            dma((2, 3)), dma((2, 3)), dma((wide_in + wide_out,)), dma((wide_in + wide_out,)),
            dma((wide_in,)), dma((wide_in,)), dma((wide_out,)), dma((wide_out,)),
            dma((2,)), dma((2,)),
        ],
        compiler_params=pltpu.CompilerParams(
            collective_id=0, has_side_effects=True, vmem_limit_bytes=56 * 1024 * 1024
        ),
    )(
        rates, test_well, log_conductivity, storage, recharge, observed,
        well_tile.reshape(1, wells), well_row.reshape(1, wells), well_col.reshape(1, wells),
        well_screen.T,
    )


def solution(mesh):
    return jax.shard_map(
        local,
        mesh=mesh,
        in_specs=(
            P("groups", "tile", None),
            P("groups", "tile", None),
            P("groups", "tile", None),
            P("groups", None),
            P("groups"),
            P(),
            P(),
            P(),
            P(),
            P(),
        ),
        out_specs=(P("groups", "tile", None), P("groups", None)),
        check_vma=False,
    )
```

```python
import functools

import jax
import jax.numpy as jnp
from jax import lax
from jax.experimental import pallas as pl
from jax.experimental.pallas import tpu as pltpu
from jax.sharding import PartitionSpec as P

ITERS = 4
HALF = 2 * ITERS + 2
WINDOW = 2 * HALF + 1
F32 = jnp.float32
BF16 = jnp.bfloat16
NT = (((1,), (1,)), ((), ()))
NN = (((1,), (0,)), ((), ()))
TN = (((0,), (0,)), ((), ()))


def split(x):
    high = x.astype(BF16)
    return high, (x - high.astype(F32)).astype(BF16)


def mxu(a, b, dims):
    return lax.dot_general(a, b, dims, preferred_element_type=F32)


def exact_left(x, picks, dims):
    both = mxu(jnp.concatenate(split(x), axis=0), picks, dims)
    return both[:x.shape[0]] + both[x.shape[0]:]


def exact_right(picks, x, dims):
    both = mxu(picks, jnp.concatenate(split(x), axis=1), dims)
    return both[:, :x.shape[1]] + both[:, x.shape[1]:]


def iota(shape, dim):
    return lax.broadcasted_iota(jnp.int32, shape, dim)


def turn(x, shift, axis):
    return pltpu.roll(x, shift % x.shape[axis], axis)


def kernel(
    n, tests, wells, *refs
):
    inputs = refs[:10]
    grad_ref, pred_ref = refs[10:12]
    held = refs[12:22]
    local_sem = refs[22]
    run(
        n, tests, wells, inputs, local_sem, *held, grad_ref, pred_ref, *refs[23:]
    )


def run(
    n, tests, wells, inputs, local_sem, rates_s, test_s,
    logc_ref, store_ref, rech_ref, obs_ref, tile_ref, row_ref, col_ref, screen_ref,
    grad_ref, pred_ref,
    halo, info, picks, near, coef, heads_ref, bounds, part, beside, inner, outer, obs_pad,
    halo_send, halo_recv, hl_send, hl_recv, in_send, in_recv, out_send, out_recv,
    side_send, side_recv,
):
    layers, strip, columns = logc_ref.shape
    assert layers == 2
    rows = 3 * strip
    both = layers * rows
    wide = info.shape[1]
    wpad = near.shape[0]
    packed = near.shape[1]
    lanes = columns + packed
    me = lax.axis_index("tile")
    held = (
        rates_s, test_s, logc_ref, store_ref, rech_ref, obs_ref, tile_ref, row_ref, col_ref,
        screen_ref,
    )
    fetches = [
        pltpu.make_async_copy(src, dst, local_sem.at[index])
        for index, (src, dst) in enumerate(zip(inputs, held))
    ]

    wide_in = inner_size(n)
    wide_out = n // wide_in
    place_in, place_out = lax.rem(me, wide_in), me // wide_in

    def inner_peer(k):
        return place_out * wide_in + lax.rem(place_in + k, wide_in)

    def outer_peer(k):
        return lax.rem(place_out + k, wide_out) * wide_in + place_in

    def remote(src, dst, send_sem, recv_sem, target):
        return pltpu.make_async_remote_copy(
            src_ref=src, dst_ref=dst, send_sem=send_sem, recv_sem=recv_sem,
            device_id={"tile": target}, device_id_type=pl.DeviceIdType.MESH,
        )

    sides = ((0, me < n - 1, me > 0, me + 1), (1, me > 0, me < n - 1, me - 1))
    barrier = pltpu.get_barrier_semaphore()

    def greet(target):
        pl.semaphore_signal(
            barrier, inc=1, device_id={"tile": target}, device_id_type=pl.DeviceIdType.MESH
        )

    next_outside = (place_in == wide_in - 1) & (me < n - 1)
    last_outside = (place_in == 0) & (me > 0)

    @pl.when(next_outside)
    def _():
        greet(me + 1)

    @pl.when(last_outside)
    def _():
        greet(me - 1)

    for k in range(1, wide_in):
        greet(inner_peer(k))
    for k in range(1, wide_out):
        greet(outer_peer(k))
    for fetch in fetches:
        fetch.start()
    outside = next_outside.astype(jnp.int32) + last_outside.astype(jnp.int32)
    pl.semaphore_wait(barrier, wide_in + wide_out - 2 + outside)
    reach = min(strip, ITERS + 1)

    def halo_copy(side, index):
        rows_sent = pl.ds(strip - reach, reach) if side == 0 else pl.ds(0, reach)
        return remote(
            inputs[2 + index].at[:, rows_sent], halo.at[side, index, :, rows_sent], halo_send.at[side, index],
            halo_recv.at[side, index], sides[side][3],
        )

    fills = (-1e30, 0.0, 0.0)
    for index in range(3):
        for side, sends, gets, target in sides:
            @pl.when(sends)
            def _():
                halo_copy(side, index).start()

    for side, sends, gets, target in sides:
        @pl.when(jnp.logical_not(gets))
        def _():
            for index in range(3):
                halo[side, index] = jnp.full((layers, strip, columns), fills[index], F32)
            beside[side] = jnp.zeros(part.shape, F32)

    for fetch in fetches:
        fetch.wait()

    info[...] = jnp.full(info.shape, -4000.0, F32)
    info[0:1, 0:wells] = col_ref[...].astype(F32)
    info[1:2, 0:wells] = ((tile_ref[...] - me) * strip + row_ref[...] + strip).astype(F32)
    info[2:4, 0:wells] = screen_ref[...].astype(F32)
    well_col = info[0:1, 0:wpad]
    well_row = info[1:2, 0:wpad]
    top = info[2:3, 0:wpad]
    bottom = info[3:4, 0:wpad]
    length = jnp.where(bottom > top, bottom - top, 1.0)
    screens = [
        jnp.where((top <= layer) & (bottom > layer), 1.0 / length, 0.0) for layer in range(layers)
    ]
    trow = iota((16, 1), 0)
    pumped = jnp.full((16, 1), -1, jnp.int32)
    rate = jnp.zeros((16, 1), F32)
    for t in range(tests):
        pumped = jnp.where(trow == t, test_s[t], pumped)
        rate = jnp.where(trow == t, rates_s[t], rate)
    chosen = iota((16, wpad), 1) == pumped

    def at_pumped(values):
        return jnp.sum(jnp.where(chosen, values, 0.0), axis=1, keepdims=True)

    slot = iota((16, packed), 1) - WINDOW * trow
    segment = (slot >= 0) & (slot < WINDOW) & (trow < tests)

    def to_lanes(column):
        return jnp.sum(jnp.where(segment, column, 0.0), axis=0, keepdims=True)

    label = jnp.sum(
        jnp.where(segment, at_pumped(well_col) - HALF + slot.astype(F32), 0.0),
        axis=0, keepdims=True,
    )
    label = jnp.where(iota((1, packed), 1) < tests * WINDOW, label, -2000.0)
    info[0:1, wpad:] = label
    pump_row = to_lanes(at_pumped(well_row))
    centre = segment & (slot == HALF)
    amounts = [
        jnp.sum(jnp.where(centre, -rate * at_pumped(screen), 0.0), axis=0, keepdims=True)
        for screen in screens
    ]
    line = iota((rows, 1), 0).astype(F32)
    pumping = jnp.concatenate(
        [jnp.where(line == pump_row, amount, 0.0) for amount in amounts], axis=0
    )
    rowsel = jnp.concatenate(
        [jnp.where(line == well_row, screen, 0.0) for screen in screens], axis=0
    )
    upright = info[...].T[:, 0:1]
    picks[...] = jnp.where(
        upright == iota((wide, columns), 1).astype(F32), 1.0, 0.0
    ).astype(BF16)
    near[...] = jnp.where(upright[0:wpad] == label, 1.0, 0.0)
    obs_pad[...] = jnp.zeros(obs_pad.shape, F32)
    obs_pad[0:tests, 0:wells] = obs_ref[...]

    def await_halo(indices):
        for side, sends, gets, target in sides:
            @pl.when(gets)
            def _():
                for index in indices:
                    halo_copy(side, index).wait_recv()

    await_halo((0,))

    def extended(ref, index):
        return jnp.concatenate(
            [
                piece
                for layer in range(layers)
                for piece in (halo[0, index, layer], ref[layer], halo[1, index, layer])
            ],
            axis=0,
        )

    cond = jnp.exp(extended(logc_ref, 0))
    line2 = lax.rem(iota((both, 1), 0), rows)
    whole_row = line2 + (me - 1) * strip
    linked = (line2 >= 1) & (whole_row >= 1) & (whole_row < n * strip)
    column = iota((1, columns), 1)
    face_up = 0.5 * (cond + turn(cond, 1, 0))
    up = jnp.where(linked, face_up, 0.0)
    left_open = 0.5 * (cond + turn(cond, 1, 1))
    left = jnp.where(column == 0, 0.0, left_open)
    face_left = jnp.where(column == 0, 0.5 * cond, left_open)
    face_right = jnp.where(column == columns - 1, 0.5 * cond, turn(left_open, -1, 1))
    across = 0.5 * (cond + turn(cond, rows, 0))
    faces = face_up + turn(face_up, -1, 0) + face_left + face_right + across

    def own(x):
        return jnp.concatenate(
            [x[layer * rows + strip:layer * rows + 2 * strip] for layer in range(layers)], axis=0
        )

    store_own = jnp.concatenate([store_ref[layer] for layer in range(layers)], axis=0)
    high_own = jnp.max(store_own + 2.0 * own(faces), keepdims=True)
    low_own = jnp.min(store_own, keepdims=True)
    bounds[0] = jnp.where(iota((1, 128), 1) < 64, high_own, -low_own)

    def bound_in(k):
        return remote(bounds.at[0], bounds.at[k], hl_send.at[k], hl_recv.at[k], inner_peer(k))

    def bound_out(k):
        at = wide_in + k
        return remote(
            bounds.at[wide_in], bounds.at[at], hl_send.at[at], hl_recv.at[at], outer_peer(k)
        )

    for k in range(1, wide_in):
        bound_in(k).start()
    await_halo((1, 2))
    store = extended(store_ref, 1)
    diag = store + faces

    for k in range(1, wide_in):
        bound_in(k).wait_recv()
    bounds[wide_in] = jnp.max(bounds[0:wide_in], axis=0)
    for k in range(1, wide_out):
        bound_out(k).start()
    stacked = jnp.concatenate([diag, up, left, across], axis=0)
    taken = exact_left(stacked, picks[wpad:, :], NT)
    for index, whole in enumerate((diag, up, left, across)):
        coef[index, :, 0:columns] = whole
        coef[index, :, columns:] = taken[index * both:(index + 1) * both]
    coef[2, :, columns:columns + 128] = jnp.where(
        iota((1, 128), 1) == 0, 0.0, taken[2 * both:3 * both, 0:128]
    )

    def operate(v):
        out = coef[0] * v - coef[1] * turn(v, 1, 0) - turn(coef[1] * v, -1, 0)
        out = out - coef[2] * turn(v, 1, 1) - turn(coef[2] * v, -1, 1)
        return out - coef[3] * turn(v, rows, 0)

    source = jnp.concatenate([extended(rech_ref, 2), pumping], axis=1)
    used = (line2 >= strip - ITERS) & (line2 < 2 * strip + ITERS)
    used = used & (whole_row >= 0) & (whole_row < n * strip)
    local_high = jnp.max(jnp.where(used, store + 2.0 * faces, 0.0), keepdims=True)
    local_low = jnp.min(jnp.where(used, store, local_high), keepdims=True)
    shift = 0.5 * (local_high + local_low)
    reduced = 0.5 * (local_high - local_low)
    inverse = 1.0 / reduced

    def scaled(v):
        return (operate(v) - shift * v) * inverse

    powers = [source, scaled(source)]
    for step in range(1, ITERS):
        powers.append(scaled(powers[-1]))
    for k in range(1, wide_out):
        bound_out(k).wait_recv()
    bound = jnp.max(bounds[wide_in:], axis=0)
    high = bound[:, 0:1]
    low = -bound[:, 64:65]
    center = 0.5 * (high + low)
    radius = 0.5 * (high - low)
    spread = center / radius

    def chebyshev(source, apply):
        ratio = 1.0 / spread
        direction = source / center
        iterate = direction
        residual = source
        for step in range(ITERS):
            residual = residual - apply(direction)
            following = 1.0 / (2.0 * spread - ratio)
            direction = (following * ratio) * direction + (2.0 * following / radius) * residual
            iterate = iterate + direction
            ratio = following
        return iterate

    unit = jnp.where(iota((1, 128), 1) == 0, 1.0, 0.0)
    weights = chebyshev(unit, lambda p: shift * p + reduced * turn(p, 1, 1))
    heads = weights[:, 0:1] * powers[0]
    for k in range(1, ITERS + 1):
        heads = heads + weights[:, k:k + 1] * powers[k]
    heads_ref[...] = heads
    mine = own(heads)
    rowsel_own = own(rowsel)
    common = jnp.sum(
        exact_left(mine[:, 0:columns], picks[0:wpad, :], NT) * rowsel_own, axis=0, keepdims=True
    )
    deltas = mine[:, columns:]
    place = iota((1, packed), 1)
    spaced = jnp.concatenate(
        [
            jnp.where((place >= t * WINDOW) & (place < (t + 1) * WINDOW), deltas, 0.0)
            for t in range(tests)
        ],
        axis=0,
    )
    read = exact_left(spaced, near[...].astype(BF16), NT)
    depth = layers * strip
    sampled = [
        jnp.sum(read[t * depth:(t + 1) * depth] * rowsel_own, axis=0, keepdims=True) + common
        for t in range(tests)
    ]
    sampled = jnp.concatenate(sampled + [jnp.zeros((16 - tests, wpad), F32)], axis=0)
    banks = wpad // 128
    for k in range(part.shape[0]):
        r, c = 4 * (k // banks), 128 * (k % banks)
        part[k] = sampled[r:r + 4, c:c + 128]

    def side_copy(side):
        return remote(
            part, beside.at[side], side_send.at[side], side_recv.at[side], sides[side][3]
        )

    def part_in(k):
        return remote(part, inner.at[k], in_send.at[k], in_recv.at[k], inner_peer(k))

    def part_out(k):
        return remote(inner.at[0], outer.at[k], out_send.at[k], out_recv.at[k], outer_peer(k))

    for side, sends, gets, target in sides:
        @pl.when(sends)
        def _():
            side_copy(side).start()

    for k in range(1, wide_in):
        part_in(k).start()
    for k in range(1, wide_in):
        part_in(k).wait_recv()
    mixed = part[...]
    for k in range(1, wide_in):
        mixed = mixed + inner[k]
    inner[0] = mixed
    for k in range(1, wide_out):
        part_out(k).start()
    for side, sends, gets, target in sides:
        @pl.when(gets)
        def _():
            side_copy(side).wait_recv()

    def assembled(x):
        bands = [
            jnp.concatenate([x[r * banks + c] for c in range(banks)], axis=1)
            for r in range(part.shape[0] // banks)
        ]
        empty = 16 - 4 * len(bands)
        return jnp.concatenate(bands + ([jnp.zeros((empty, wpad), F32)] if empty else []), axis=0)

    valid = (iota((16, wpad), 0) < tests) & (iota((16, wpad), 1) < wells)
    misfit = assembled(part[...] + beside[0] + beside[1]) - obs_pad[...]
    misfit = jnp.where(valid, misfit, 0.0)

    summed = jnp.sum(misfit, axis=0, keepdims=True)
    dense = exact_left(rowsel * summed, picks[0:wpad, :], NN)
    segment_f = jnp.where(segment, 1.0, 0.0).astype(BF16)
    spread_weight = mxu(
        jnp.concatenate(split(misfit), axis=0),
        jnp.concatenate([segment_f, segment_f], axis=0), TN,
    )
    placed = exact_right(rowsel.astype(BF16), spread_weight * near[...], NN)
    source = jnp.concatenate([dense, placed], axis=1)
    adjoint = chebyshev(source, operate)

    heads = heads_ref[...]
    lane = iota((1, lanes), 1)
    start = (lane == 0) | (lane == columns)

    def before(x):
        return jnp.where(start, 0.0, turn(x, 1, 1))

    term_x = 0.5 * (adjoint - turn(adjoint, 1, 0)) * (heads - turn(heads, 1, 0))
    x_sum = term_x + turn(term_x, -1, 0)
    term_y = 0.5 * (adjoint - before(adjoint)) * (heads - before(heads))
    term_right = jnp.where(
        lane == columns - 1, 0.5 * adjoint * heads, turn(term_y, -1, 1)
    )
    term_z = 0.5 * (adjoint - turn(adjoint, rows, 0)) * (heads - turn(heads, rows, 0))
    cells = own(x_sum + term_y + term_right + term_z)
    cells = cells[:, 0:columns] + exact_left(cells[:, columns:], picks[wpad:, :], NN)
    for k in range(1, wide_out):
        part_out(k).wait_recv()
    total = inner[0]
    for k in range(1, wide_out):
        total = total + outer[k]
    predicted = assembled(total)
    pred_ref[...] = predicted[0:tests, 0:wells]
    misfit = jnp.where(valid, predicted - obs_pad[...], 0.0)
    square = jnp.sum(misfit * misfit, keepdims=True)
    gain = -1.0 / jnp.sqrt(square / (tests * wells) + 1e-06)
    for layer in range(layers):
        grad_ref[layer] = jnp.exp(logc_ref[layer]) * (
            gain * cells[layer * strip:(layer + 1) * strip]
        )

    for side, sends, gets, target in sides:
        @pl.when(sends)
        def _():
            for index in range(3):
                halo_copy(side, index).wait_send()
            side_copy(side).wait_send()

    for k in range(1, wide_in):
        bound_in(k).wait_send()
        part_in(k).wait_send()
    for k in range(1, wide_out):
        bound_out(k).wait_send()
        part_out(k).wait_send()


def inner_size(n):
    size = 1
    while 4 * size * size <= n and n % (2 * size) == 0:
        size *= 2
    return size


def round_up(value, unit):
    return -(-value // unit) * unit


def local(
    log_conductivity, storage, recharge, observed, rates,
    well_tile, well_row, well_col, well_screen, test_well,
):
    layers, strip, columns = log_conductivity.shape
    tests, wells = observed.shape
    n = lax.axis_size("tile")
    wpad = round_up(wells, 128)
    packed = round_up(tests * WINDOW, 128)
    both = layers * 3 * strip
    lanes = columns + packed
    slots = round_up(tests, 4) // 4 * (wpad // 128)
    wide_in = inner_size(n)
    wide_out = n // wide_in
    vmem = pl.BlockSpec(memory_space=pltpu.VMEM)
    dma = pltpu.SemaphoreType.DMA
    return pl.pallas_call(
        functools.partial(kernel, n, tests, wells),
        out_shape=(
            jax.ShapeDtypeStruct((layers, strip, columns), F32),
            jax.ShapeDtypeStruct((tests, wells), F32),
        ),
        in_specs=[pl.BlockSpec(memory_space=pl.ANY)] * 10,
        out_specs=(vmem, vmem),
        scratch_shapes=[
            pltpu.SMEM((tests,), F32),
            pltpu.SMEM((tests,), jnp.int32),
            pltpu.VMEM((layers, strip, columns), F32),
            pltpu.VMEM((layers, strip, columns), F32),
            pltpu.VMEM((layers, strip, columns), F32),
            pltpu.VMEM((tests, wells), F32),
            pltpu.VMEM((1, wells), jnp.int32),
            pltpu.VMEM((1, wells), jnp.int32),
            pltpu.VMEM((1, wells), jnp.int32),
            pltpu.VMEM((2, wells), jnp.int32),
            dma((10,)),
            pltpu.VMEM((2, 3, layers, strip, columns), F32),
            pltpu.VMEM((8, wpad + packed), F32),
            pltpu.VMEM((wpad + packed, columns), BF16),
            pltpu.VMEM((wpad, packed), F32),
            pltpu.VMEM((4, both, lanes), F32),
            pltpu.VMEM((both, lanes), F32),
            pltpu.VMEM((wide_in + wide_out, 1, 128), F32),
            pltpu.VMEM((slots, 4, 128), F32),
            pltpu.VMEM((2, slots, 4, 128), F32),
            pltpu.VMEM((wide_in, slots, 4, 128), F32),
            pltpu.VMEM((wide_out, slots, 4, 128), F32),
            pltpu.VMEM((16, wpad), F32),
            dma((2, 3)), dma((2, 3)), dma((wide_in + wide_out,)), dma((wide_in + wide_out,)),
            dma((wide_in,)), dma((wide_in,)), dma((wide_out,)), dma((wide_out,)),
            dma((2,)), dma((2,)),
        ],
        compiler_params=pltpu.CompilerParams(
            collective_id=0, has_side_effects=True, vmem_limit_bytes=56 * 1024 * 1024
        ),
    )(
        rates, test_well, log_conductivity, storage, recharge, observed,
        well_tile.reshape(1, wells), well_row.reshape(1, wells), well_col.reshape(1, wells),
        well_screen.T,
    )


def solution(mesh):
    return jax.shard_map(
        local,
        mesh=mesh,
        in_specs=(
            P("groups", "tile", None),
            P("groups", "tile", None),
            P("groups", "tile", None),
            P("groups", None),
            P("groups"),
            P(),
            P(),
            P(),
            P(),
            P(),
        ),
        out_specs=(P("groups", "tile", None), P("groups", None)),
        check_vma=False,
    )
```
